128 devices in a mesh: dp: 8 (over z, core), tensor: 16 (over x, y).
Axes of the slice: x: 4, y: 4, z: 4, core: 2. Of those that a mesh axis runs over, the one named last changes fastest.
Arguments:
- activations: float32 [512, 32, 16384], P('dp', None, 'tensor'), may hold values from -6 to 6
- gradients: float32 [512, 32, 16384], P('dp', None, 'tensor'), may hold values from -6 to 6
- proj_in: float32 [16384, 128], P('tensor'), may hold values from -0.046875 to 0.046875
- proj_out: float32 [16384, 128], P('tensor'), may hold values from -0.046875 to 0.046875
- damping: float32 [16384], P(('dp', 'tensor')), may hold values from 1 to 100
- queries: float32 [16384, 512], P(('dp', 'tensor')), may hold values from -6 to 6
Outputs:
- solution: float32 [16384, 512], P(('dp', 'tensor'))
- residual: float32 [16384, 512], P(('dp', 'tensor'))
- gram: float32 [16384, 8, 2048], P('dp', None, 'tensor')
The draws below stay inside these ranges and needn't reach their ends.
All inputs are finite; a program needn't handle non-finite values. Where the reference program divides by a largest or mean magnitude, that divisor is 1e-20 or more.
Results may differ from the reference program's by a relative error of at most 0.00013.
Values sent between devices are 32-bit elements; how exact they have to be, the bound alone decides.
A program may use at most 128 MiB of HBM per device.

```python
import math
import jax
import jax.numpy as jnp
from jax import lax

DIN = 16384
DOUT = 16384
RANK = 128
TOKLEN = 32
QUERIES = 512
ITERS = 2
SEQS = 512
FEAT = 16384
GRID = 8
BLOCK = 2048


def block_scale(own_key, shape, split, smallest, largest):
    def one(position, parts):
        steps = jax.random.uniform(jax.random.fold_in(jax.random.fold_in(own_key, 6), position), (parts,), jnp.float32, smallest / len(split), largest / len(split))
        return jnp.repeat(jnp.exp(steps), shape[position] // parts).reshape((-1,) + (1,) * (len(shape) - position - 1))

    factor_of = one(*split[0])
    for cut in split[1:]:
        factor_of = factor_of * one(*cut)
    return factor_of


def normal_values(own_key, extent, spread, most, pieces=(), held_as=jnp.bfloat16):
    array = jax.random.normal(own_key, extent, jnp.float32) * spread
    if len(pieces) > 0:
        array = block_scale(own_key, extent, pieces, -0.22, 0.18) * array
    return jnp.clip(array, min=-most, max=most).astype(held_as)


def setup_inputs(seed: int = 0) -> dict:
    key_list = jax.random.split(jax.random.key(seed), 7)
    return {
        "activations": normal_values(key_list[0], (SEQS, TOKLEN, DIN), 1.0, 6.0, ((0, 8), (2, 16)), jnp.float32),
        "gradients": normal_values(key_list[1], (SEQS, TOKLEN, DOUT), 1.0, 6.0, ((0, 8), (2, 16)), jnp.float32),
        "proj_in": normal_values(key_list[2], (DIN, RANK), DIN ** -0.5, 0.046875, ((0, 16),), jnp.float32),
        "proj_out": normal_values(key_list[3], (DOUT, RANK), DOUT ** -0.5, 0.046875, ((0, 16),), jnp.float32),
        "damping": jnp.clip(jnp.exp(math.log(100.0) - 4.6051702 * jax.random.uniform(key_list[4], (FEAT,), jnp.float32) ** block_scale(key_list[4], (FEAT,), ((0, 128),), -0.2, 0.2)), 1.0, 100.0),
        "queries": normal_values(key_list[5], (FEAT, QUERIES), 1.0, 6.0, ((0, 128),), jnp.float32),
    }


HIGHEST = lax.Precision.HIGHEST


def reference(activations, gradients, proj_in, proj_out, damping, queries):
    act_rows = activations.reshape(SEQS * TOKLEN, DIN)
    grad_rows = gradients.reshape(SEQS * TOKLEN, DOUT)
    proj_acts = jnp.dot(act_rows, proj_in, precision=HIGHEST, preferred_element_type=jnp.float32).reshape(SEQS, TOKLEN, RANK)
    proj_grads = jnp.dot(grad_rows, proj_out, precision=HIGHEST, preferred_element_type=jnp.float32).reshape(SEQS, TOKLEN, RANK)
    features = jnp.einsum("sti,stj->sij", proj_grads, proj_acts, precision=HIGHEST).reshape(SEQS, RANK * RANK)
    gram_full = jnp.einsum("sr,sc->rc", features, features, precision=HIGHEST) / SEQS
    bound_high = jnp.max(jnp.sum(jnp.abs(gram_full), axis=1) + damping)
    bound_low = jnp.min(damping)

    def operate(direction):
        applied = jnp.dot(gram_full, direction, precision=HIGHEST) + damping[:, None] * direction
        return applied / bound_high

    ratio_low = bound_low / bound_high
    center_value = (1.0 + ratio_low) / 2.0
    half_width = (1.0 - ratio_low) / 2.0
    spread_ratio = center_value / half_width
    ratio_now = 1.0 / spread_ratio
    solution = jnp.zeros_like(queries)
    residual = queries
    direction = queries / center_value
    for iteration in range(ITERS):
        solution = solution + direction
        residual = residual - operate(direction)
        if iteration + 1 < ITERS:
            ratio_next = 1.0 / (2.0 * spread_ratio - ratio_now)
            direction = ratio_next * ratio_now * direction + (2.0 * ratio_next / half_width) * residual
            ratio_now = ratio_next
    return solution, residual, gram_full.reshape(FEAT, GRID, BLOCK)
```

```python
import jax
import jax.numpy as jnp
from jax import lax
from jax.experimental import pallas as pl
from jax.experimental.pallas import tpu as pltpu
from jax.sharding import PartitionSpec as P

MESH = pl.DeviceIdType.MESH
F32 = jnp.float32
BF16 = jnp.bfloat16
ORDER = (1, 3, 2)
NT = (((1,), (1,)), ((), ()))
NN = (((1,), (0,)), ((), ()))
TN = (((0,), (0,)), ((), ()))


def vmem():
    return pl.BlockSpec(memory_space=pltpu.VMEM)


def hbm():
    return pl.BlockSpec(memory_space=pl.ANY)


def params(collective_id, mib):
    return pltpu.CompilerParams(
        collective_id=collective_id, has_side_effects=True, vmem_limit_bytes=mib * 2**20
    )


def place():
    d, t = lax.axis_index("dp"), lax.axis_index("tensor")
    return d, t, lax.div(d, 2), lax.rem(d, 2), lax.div(t, 4), lax.rem(t, 4)


def shift(value, by, size):
    return lax.rem(value + by, size)


def greet(peers):
    barrier = pltpu.get_barrier_semaphore()
    for peer in peers:
        pl.semaphore_signal(barrier, inc=1, device_id=peer, device_id_type=MESH)


def greeted(count):
    pl.semaphore_wait(pltpu.get_barrier_semaphore(), count)


def send(src, dst, send_sem, recv_sem, peer):
    copy = pltpu.make_async_remote_copy(
        src_ref=src,
        dst_ref=dst,
        send_sem=send_sem,
        recv_sem=recv_sem,
        device_id=peer,
        device_id_type=MESH,
    )
    copy.start()
    return copy


def parts(value):
    high = value.astype(BF16)
    low = (value - high.astype(F32)).astype(BF16)
    return high, low


def mm(a, b, dims):
    return lax.dot_general(a, b, dims, preferred_element_type=F32)


def few_rows(value, weight_high, weight_low, dims):
    rows = value.shape[0]
    high, low = parts(value)
    both = mm(jnp.concatenate((high, low), axis=0), weight_high, dims)
    return both[:rows] + both[rows:] + mm(high, weight_low, dims)


def project_kernel(
    act, grad, pin, pout, q, damp, fd, qr,
    gbuf, abuf, wg, wa, yg, ya, r1g, r1a, s2g, s2a, r2g, r2a, qs, fsend, frecv,
    in_sem, s1_sem, r1_sem, s2_sem, r2_sem, sq_sem, rq_sem, sf_sem, rf_sem,
):
    d, t, z, c, x, y = place()
    loads = []
    for n, o in enumerate(ORDER + (0,)):
        g = pltpu.make_async_copy(grad.at[shift(x, o, 4)], gbuf.at[n], in_sem.at[0, n])
        a = pltpu.make_async_copy(act.at[:, shift(y, o, 4)], abuf.at[n], in_sem.at[1, n])
        g.start()
        a.start()
        loads.append((g, a))
    peers = [(d, shift(t, o, 16)) for o in range(1, 16)]
    greet(peers)
    row = lax.broadcasted_iota(jnp.int32, (128, 128), 0)
    column = lax.broadcasted_iota(jnp.int32, (128, 128), 1)
    order = (row == 16 * lax.rem(column, 8) + lax.div(column, 8)).astype(BF16)
    high, low = parts(pout[...])
    wg[:, :128] = mm(high, order, NN).astype(BF16)
    wg[:, 128:] = mm(low, order, NN).astype(BF16)
    high, low = parts(pin[...])
    wa[:, :128] = high
    wa[:, 128:] = low
    for n in range(16):
        qs[n, :32] = q[:, pl.ds(128 * (n // 4), 128)].T[32 * (n % 4) : 32 * (n % 4) + 32]
        qs[n, 32:] = jnp.broadcast_to(damp[...], (8, 128))
    greeted(15)
    copies = []
    for n in range(15):
        to = shift(t, n + 1, 16)
        copies.append(send(qs.at[to], qr.at[t], sq_sem.at[n], rq_sem.at[n], (d, to)))
    qr[t] = qs[t]

    def project(buf, weight, out, n):
        def step(m, carry):
            high, low = parts(buf[n, m])
            first = mm(high, weight[...], NN)
            second = mm(low, weight[:, :128], NN)
            out[n, m] = first[:, :128] + first[:, 128:] + second
            return carry

        lax.fori_loop(0, 4, step, 0)

    firsts = []
    for n, o in enumerate(ORDER + (0,)):
        loads[n][0].wait()
        project(gbuf, wg, yg, n)
        if o:
            firsts.append(
                send(yg.at[n], r1g.at[n], s1_sem.at[0, n], r1_sem.at[0, n], (d, shift(x, o, 4) * 4 + y))
            )
        loads[n][1].wait()
        project(abuf, wa, ya, n)
        if o:
            firsts.append(
                send(ya.at[n], r1a.at[n], s1_sem.at[1, n], r1_sem.at[1, n], (d, x * 4 + shift(y, o, 4)))
            )
    for copy in firsts:
        copy.wait()

    def total(own, got, at):
        return own[3, at] + got[0, at] + (got[1, at] + got[2, at])

    seconds = []
    for n, o in enumerate(ORDER):
        yy, xx = shift(y, o, 4), shift(x, o, 4)
        s2g[n] = total(yg, r1g, yy)
        seconds.append(send(s2g.at[n], r2g.at[n], s2_sem.at[0, n], r2_sem.at[0, n], (d, x * 4 + yy)))
        s2a[n] = total(ya, r1a, xx)
        seconds.append(send(s2a.at[n], r2a.at[n], s2_sem.at[1, n], r2_sem.at[1, n], (d, xx * 4 + y)))
    pg = total(yg, r1g, y)
    pa = total(ya, r1a, x)
    for copy in seconds:
        copy.wait()
    pg = pg + r2g[0] + (r2g[1] + r2g[2])
    pa = pa + r2a[0] + (r2a[1] + r2a[2])
    for s in range(4):
        gh, gl = parts(pg[32 * s : 32 * s + 32].T)
        ah, al = parts(pa[32 * s : 32 * s + 32])
        feature = mm(gh, ah, NN) + mm(gh, al, NN) + mm(gl, ah, NN)
        fsend[:, s] = feature.reshape(16, 8, 128)
    for n in range(15):
        to = shift(t, n + 1, 16)
        copies.append(send(fsend.at[to], frecv.at[t], sf_sem.at[n], rf_sem.at[n], (d, to)))
    frecv[t] = fsend[t]
    for copy in copies:
        copy.wait()
    for k in range(8):
        fd[k] = frecv[:, :, k, :].reshape(64, 128)


def project(act, grad, pin, pout, q, damp):
    sem = pltpu.SemaphoreType.DMA
    return pl.pallas_call(
        project_kernel,
        out_shape=(
            jax.ShapeDtypeStruct((8, 64, 128), F32),
            jax.ShapeDtypeStruct((16, 40, 128), F32),
        ),
        in_specs=[hbm(), hbm(), vmem(), vmem(), vmem(), vmem()],
        out_specs=(vmem(), vmem()),
        scratch_shapes=[
            pltpu.VMEM((4, 4, 128, 1024), F32),
            pltpu.VMEM((4, 4, 128, 1024), F32),
            pltpu.VMEM((1024, 256), BF16),
            pltpu.VMEM((1024, 256), BF16),
            pltpu.VMEM((4, 4, 128, 128), F32),
            pltpu.VMEM((4, 4, 128, 128), F32),
            pltpu.VMEM((3, 4, 128, 128), F32),
            pltpu.VMEM((3, 4, 128, 128), F32),
            pltpu.VMEM((3, 128, 128), F32),
            pltpu.VMEM((3, 128, 128), F32),
            pltpu.VMEM((3, 128, 128), F32),
            pltpu.VMEM((3, 128, 128), F32),
            pltpu.VMEM((16, 40, 128), F32),
            pltpu.VMEM((16, 4, 8, 128), F32),
            pltpu.VMEM((16, 4, 8, 128), F32),
            sem((2, 4)),
            sem((2, 3)),
            sem((2, 3)),
            sem((2, 3)),
            sem((2, 3)),
            sem((15,)),
            sem((15,)),
            sem((15,)),
            sem((15,)),
        ],
        compiler_params=params(1, 56),
    )(act, grad, pin, pout, q, damp)


def gather_kernel(fd, rows, cols, slab, s1, r1, sc, rc, sx, rx, s3, r3):
    d, t, z, c, x, y = place()
    dp_peers = [(shift(d, o, 8), t) for o in range(1, 8)]
    xs = [(d, shift(x, o, 4) * 4 + y) for o in ORDER]
    ys = [(d, x * 4 + shift(y, o, 4)) for o in ORDER]
    greet(dp_peers + xs + ys)
    greeted(13)
    firsts = []
    for n in range(7):
        to = shift(d, n + 1, 8)
        firsts.append(send(fd.at[to], slab.at[d], s1.at[n], r1.at[n], (to, t)))
    slab[d] = fd[d]
    cols[d] = fd[...]
    zs = [send(fd, cols.at[d], sc.at[n], rc.at[n], (shift(z, o, 4) * 2 + c, t)) for n, o in enumerate(ORDER)]
    other = (z * 2 + 1 - c, t)
    cores = [send(fd, cols.at[d], sx.at[3], rx.at[3], other)]
    for copy in firsts:
        copy.wait()
    for n in range(4):
        piece = slab[2 * n : 2 * n + 2].reshape(128, 128).T
        rows[t, 0, :, 128 * n : 128 * n + 128] = piece[:64]
        rows[t, 1, :, 128 * n : 128 * n + 128] = piece[64:]

    def hop(half, at, first, second, peer):
        return send(
            rows.at[at, half], rows.at[at, half], s3.at[half, first, second], r3.at[half, first, second], peer
        )

    firsts, rest = {}, []
    for n in range(3):
        firsts[0, n] = hop(0, t, n, 3, xs[n])
        firsts[1, n] = hop(1, t, n, 3, ys[n])
    for n in range(3):
        rest.append(hop(0, t, 3, n, ys[n]))
        rest.append(hop(1, t, 3, n, xs[n]))
    for n, o in enumerate(ORDER):
        firsts[0, n].wait()
        for m in range(3):
            rest.append(hop(0, shift(x, 4 - o, 4) * 4 + y, n, m, ys[m]))
        firsts[1, n].wait()
        for m in range(3):
            rest.append(hop(1, x * 4 + shift(y, 4 - o, 4), n, m, xs[m]))
    for n, o in enumerate(ORDER):
        zs[n].wait()
        from_d = shift(z, 4 - o, 4) * 2 + c
        cores.append(send(cols.at[from_d], cols.at[from_d], sx.at[n], rx.at[n], other))
    for copy in cores + rest:
        copy.wait()


def gather(fd):
    sem = pltpu.SemaphoreType.DMA
    return pl.pallas_call(
        gather_kernel,
        out_shape=(
            jax.ShapeDtypeStruct((16, 2, 64, 512), F32),
            jax.ShapeDtypeStruct((8, 8, 64, 128), F32),
        ),
        in_specs=[vmem()],
        out_specs=(vmem(), vmem()),
        scratch_shapes=[
            pltpu.VMEM((8, 64, 128), F32),
            sem((7,)),
            sem((7,)),
            sem((3,)),
            sem((3,)),
            sem((4,)),
            sem((4,)),
            sem((2, 4, 4)),
            sem((2, 4, 4)),
        ],
        compiler_params=params(2, 40),
    )(fd)


def gram_kernel(rows, cols, qr, gram, sums, fq, rows_high, rows_low, ch, cl):
    step = pl.program_id(0)

    @pl.when(step == 0)
    def _():
        def fill(n, carry):
            at = pl.ds(pl.multiple_of(n * 64, 64), 64)
            for k in range(8):
                high, low = parts(cols[n, k] * (1.0 / 512))
                ch[at, 128 * k : 128 * k + 128] = high
                cl[at, 128 * k : 128 * k + 128] = low
            return carry

        lax.fori_loop(0, 8, fill, 0)
        fq[...] = jnp.zeros_like(fq)

    high, low = parts(rows[...])
    rows_high[...] = high
    rows_low[...] = low
    total = jnp.zeros((256, 128), F32)
    for k in range(4):
        at = pl.ds(256 * k, 256)
        tile = mm(high, ch[:, at], NN) + mm(high, cl[:, at], NN) + mm(low, ch[:, at], NN)
        gram[:, 2 * k, :] = tile[:, :128]
        gram[:, 2 * k + 1, :] = tile[:, 128:]
        total = total + jnp.abs(tile[:, :128]) + jnp.abs(tile[:, 128:])
    sums[0, 0] = jnp.sum(total[:128].T, axis=0)
    sums[0, 1] = jnp.sum(total[128:].T, axis=0)
    query = jnp.concatenate((qr[0, :32], qr[1, :32]), axis=1)
    fq[...] += few_rows(query, high, low, NN)


def gram_tile(rows, cols, qr):
    return pl.pallas_call(
        gram_kernel,
        grid=(8,),
        out_shape=(
            jax.ShapeDtypeStruct((2048, 8, 128), F32),
            jax.ShapeDtypeStruct((8, 2, 128), F32),
            jax.ShapeDtypeStruct((32, 512), F32),
            jax.ShapeDtypeStruct((2048, 512), BF16),
            jax.ShapeDtypeStruct((2048, 512), BF16),
        ),
        in_specs=[
            pl.BlockSpec((256, 512), lambda n: (n, 0)),
            pl.BlockSpec((8, 8, 64, 128), lambda n: (0, 0, 0, 0)),
            pl.BlockSpec((2, 40, 128), lambda n: (n, 0, 0)),
        ],
        out_specs=(
            pl.BlockSpec((256, 8, 128), lambda n: (n, 0, 0)),
            pl.BlockSpec((1, 2, 128), lambda n: (n, 0, 0)),
            pl.BlockSpec((32, 512), lambda n: (0, 0)),
            pl.BlockSpec((256, 512), lambda n: (n, 0)),
            pl.BlockSpec((256, 512), lambda n: (n, 0)),
        ),
        scratch_shapes=[pltpu.VMEM((512, 1024), BF16), pltpu.VMEM((512, 1024), BF16)],
        compiler_params=pltpu.CompilerParams(vmem_limit_bytes=40 * 2**20),
    )(rows, cols, qr)


def solve_kernel(
    rows_high, rows_low, fq, sums, qr, sol, res,
    fp, got1, got2, sums_all, pt, mine, bounds, out, back,
    s_fq, r_fq, s_fp, r_fp, s_sum, r_sum, s_bound, r_bound, s_out, r_out,
):
    d, t, z, c, x, y = place()
    dp_peers = [(shift(d, o, 8), t) for o in range(1, 8)]
    tensor_peers = [(d, shift(t, o, 16)) for o in range(1, 16)]
    greet(dp_peers + tensor_peers)
    greeted(22)
    copies = [send(fq, got1.at[n], s_fq.at[n], r_fq.at[n], peer) for n, peer in enumerate(dp_peers)]
    sum_copies = [
        send(sums, sums_all.at[n], s_sum.at[n], r_sum.at[n], peer) for n, peer in enumerate(tensor_peers)
    ]
    for copy in copies:
        copy.wait()
    fq_all = fq[...]
    for n in range(7):
        fq_all = fq_all + got1[n]
    fp[...] = jnp.zeros_like(fp)

    def forward(n, carry):
        at = pl.ds(pl.multiple_of(n * 256, 256), 256)
        product = few_rows(fq_all, rows_high[at], rows_low[at], NT) * (1.0 / 512)
        for h in range(2):
            pt[2 * n + h] = product[:, 128 * h : 128 * h + 128] + qr[2 * n + h, 32:33] * qr[2 * n + h, :32]
        value = jnp.concatenate((pt[2 * n], pt[2 * n + 1]), axis=1)
        fp[...] += few_rows(value, rows_high[at], rows_low[at], NN)
        return carry

    lax.fori_loop(0, 8, forward, 0)
    copies = [send(fp, got2.at[n], s_fp.at[n], r_fp.at[n], peer) for n, peer in enumerate(dp_peers)]
    for copy in sum_copies:
        copy.wait()
    row_sums = sums[...]
    for n in range(15):
        row_sums = row_sums + sums_all[n]
    damping = qr[:, 32:33].reshape(16, 128)
    high = jnp.max(row_sums.reshape(16, 128) + damping, axis=(0, 1), keepdims=True)
    low = jnp.min(damping, axis=(0, 1), keepdims=True)
    mine[:8] = jnp.broadcast_to(high, (8, 128))
    mine[8:] = jnp.broadcast_to(low, (8, 128))
    bound_copies = [
        send(mine, bounds.at[n], s_bound.at[n], r_bound.at[n], peer) for n, peer in enumerate(dp_peers)
    ]
    for copy in bound_copies:
        copy.wait()
    bound_high, bound_low = mine[:1], mine[8:9]
    for n in range(7):
        bound_high = jnp.maximum(bound_high, bounds[n, :1])
        bound_low = jnp.minimum(bound_low, bounds[n, 8:9])
    ratio_low = bound_low / bound_high
    center = (1.0 + ratio_low) / 2.0
    half = (1.0 - ratio_low) / 2.0
    spread = center / half
    ratio = 1.0 / spread
    ratio_next = 1.0 / (2.0 * spread - ratio)
    keep = ratio_next * ratio
    add = 2.0 * ratio_next / half
    for copy in copies:
        copy.wait()
    fp_all = fp[...]
    for n in range(7):
        fp_all = fp_all + got2[n]
    fp_all = fp_all / jnp.concatenate([bound_high] * 4, axis=1)

    def finish(n, carry):
        at = pl.ds(pl.multiple_of(n * 256, 256), 256)
        product = few_rows(fp_all, rows_high[at], rows_low[at], NT) * (1.0 / 512)
        for h in range(2):
            query, damp = qr[2 * n + h, :32], qr[2 * n + h, 32:33]
            scaled = pt[2 * n + h] / bound_high
            used = scaled / center
            first = query / center
            residual = query - used
            second = keep * first + add * residual
            out[2 * n + h, 0] = first + second
            applied = (product[:, 128 * h : 128 * h + 128] / center + damp * used) / bound_high
            out[2 * n + h, 1] = residual - (keep * used + add * (scaled - applied))
        return carry

    lax.fori_loop(0, 8, finish, 0)
    copies = []
    for n in range(15):
        to = shift(t, n + 1, 16)
        copies.append(send(out.at[to], back.at[t], s_out.at[n], r_out.at[n], (d, to)))
    back[t] = out[t]
    for copy in copies:
        copy.wait()
    for n in range(4):
        sol[:, 128 * n : 128 * n + 128] = back[4 * n : 4 * n + 4, 0].reshape(128, 128).T
        res[:, 128 * n : 128 * n + 128] = back[4 * n : 4 * n + 4, 1].reshape(128, 128).T


def solve(rows_high, rows_low, fq, sums, qr):
    sem = pltpu.SemaphoreType.DMA
    return pl.pallas_call(
        solve_kernel,
        out_shape=(jax.ShapeDtypeStruct((128, 512), F32), jax.ShapeDtypeStruct((128, 512), F32)),
        in_specs=[vmem()] * 5,
        out_specs=(vmem(), vmem()),
        scratch_shapes=[
            pltpu.VMEM((32, 512), F32),
            pltpu.VMEM((7, 32, 512), F32),
            pltpu.VMEM((7, 32, 512), F32),
            pltpu.VMEM((15, 16, 128), F32),
            pltpu.VMEM((16, 32, 128), F32),
            pltpu.VMEM((16, 128), F32),
            pltpu.VMEM((7, 16, 128), F32),
            pltpu.VMEM((16, 2, 32, 128), F32),
            pltpu.VMEM((16, 2, 32, 128), F32),
            sem((7,)),
            sem((7,)),
            sem((7,)),
            sem((7,)),
            sem((15,)),
            sem((15,)),
            sem((7,)),
            sem((7,)),
            sem((15,)),
            sem((15,)),
        ],
        compiler_params=params(3, 40),
    )(rows_high, rows_low, fq, sums, qr)


def shards(activations, gradients, proj_in, proj_out, damping, queries):
    act = activations.reshape(4, 4, 128, 1024)
    grad = gradients.reshape(4, 4, 128, 1024)
    fd, qr = project(act, grad, proj_in, proj_out, queries, damping.reshape(1, 128))
    rows, cols = gather(fd)
    gram, sums, fq, rows_high, rows_low = gram_tile(rows.reshape(2048, 512), cols, qr)
    answer, residual = solve(rows_high, rows_low, fq, sums.reshape(16, 128), qr)
    return answer, residual, gram


def solution(mesh):
    return jax.shard_map(
        shards,
        mesh=mesh,
        in_specs=(
            P("dp", None, "tensor"),
            P("dp", None, "tensor"),
            P("tensor", None),
            P("tensor", None),
            P(("dp", "tensor")),
            P(("dp", "tensor"), None),
        ),
        out_specs=(P(("dp", "tensor"), None), P(("dp", "tensor"), None), P("dp", None, "tensor")),
        check_vma=False,
    )
```

```python
import jax
import jax.numpy as jnp
from jax import lax
from jax.experimental import pallas as pl
from jax.experimental.pallas import tpu as pltpu
from jax.sharding import PartitionSpec as P

MESH = pl.DeviceIdType.MESH
F32 = jnp.float32
BF16 = jnp.bfloat16
ORDER = (1, 3, 2)
NT = (((1,), (1,)), ((), ()))
NN = (((1,), (0,)), ((), ()))
TN = (((0,), (0,)), ((), ()))


def vmem():
    return pl.BlockSpec(memory_space=pltpu.VMEM)


def hbm():
    return pl.BlockSpec(memory_space=pl.ANY)


def params(collective_id, mib):
    return pltpu.CompilerParams(
        collective_id=collective_id, has_side_effects=True, vmem_limit_bytes=mib * 2**20
    )


def place():
    d, t = lax.axis_index("dp"), lax.axis_index("tensor")
    return d, t, lax.div(d, 2), lax.rem(d, 2), lax.div(t, 4), lax.rem(t, 4)


def shift(value, by, size):
    return lax.rem(value + by, size)


def greet(peers):
    barrier = pltpu.get_barrier_semaphore()
    for peer in peers:
        pl.semaphore_signal(barrier, inc=1, device_id=peer, device_id_type=MESH)


def greeted(count):
    pl.semaphore_wait(pltpu.get_barrier_semaphore(), count)


def send(src, dst, send_sem, recv_sem, peer):
    copy = pltpu.make_async_remote_copy(
        src_ref=src,
        dst_ref=dst,
        send_sem=send_sem,
        recv_sem=recv_sem,
        device_id=peer,
        device_id_type=MESH,
    )
    copy.start()
    return copy


def parts(value):
    high = value.astype(BF16)
    low = (value - high.astype(F32)).astype(BF16)
    return high, low


def mm(a, b, dims):
    return lax.dot_general(a, b, dims, preferred_element_type=F32)


def few_rows(value, weight_high, weight_low, dims):
    rows = value.shape[0]
    high, low = parts(value)
    both = mm(jnp.concatenate((high, low), axis=0), weight_high, dims)
    return both[:rows] + both[rows:] + mm(high, weight_low, dims)


def project_kernel(
    act, grad, pin, pout, q, damp, fd, qr,
    gbuf, abuf, wg, wa, yg, ya, r1g, r1a, s2g, s2a, r2g, r2a, qs, fsend, frecv,
    in_sem, s1_sem, r1_sem, s2_sem, r2_sem, sq_sem, rq_sem, sf_sem, rf_sem,
):
    d, t, z, c, x, y = place()
    loads = []
    for n, o in enumerate(ORDER + (0,)):
        g = pltpu.make_async_copy(grad.at[shift(x, o, 4)], gbuf.at[n], in_sem.at[0, n])
        a = pltpu.make_async_copy(act.at[:, shift(y, o, 4)], abuf.at[n], in_sem.at[1, n])
        g.start()
        a.start()
        loads.append((g, a))
    peers = [(d, shift(t, o, 16)) for o in range(1, 16)]
    greet(peers)
    row = lax.broadcasted_iota(jnp.int32, (128, 128), 0)
    column = lax.broadcasted_iota(jnp.int32, (128, 128), 1)
    order = (row == 16 * lax.rem(column, 8) + lax.div(column, 8)).astype(BF16)
    high, low = parts(pout[...])
    wg[:, :128] = mm(high, order, NN).astype(BF16)
    wg[:, 128:] = mm(low, order, NN).astype(BF16)
    high, low = parts(pin[...])
    wa[:, :128] = high
    wa[:, 128:] = low
    for n in range(16):
        qs[n, :32] = q[:, pl.ds(128 * (n // 4), 128)].T[32 * (n % 4) : 32 * (n % 4) + 32]
        qs[n, 32:] = jnp.broadcast_to(damp[...], (8, 128))
    greeted(15)
    copies = []
    for n in range(15):
        to = shift(t, n + 1, 16)
        copies.append(send(qs.at[to], qr.at[t], sq_sem.at[n], rq_sem.at[n], (d, to)))
    qr[t] = qs[t]

    def project(buf, weight, out, n):
        def step(m, carry):
            high, low = parts(buf[n, m])
            first = mm(high, weight[...], NN)
            second = mm(low, weight[:, :128], NN)
            out[n, m] = first[:, :128] + first[:, 128:] + second
            return carry

        lax.fori_loop(0, 4, step, 0)

    firsts = []
    for n, o in enumerate(ORDER + (0,)):
        loads[n][0].wait()
        project(gbuf, wg, yg, n)
        if o:
            firsts.append(
                send(yg.at[n], r1g.at[n], s1_sem.at[0, n], r1_sem.at[0, n], (d, shift(x, o, 4) * 4 + y))
            )
        loads[n][1].wait()
        project(abuf, wa, ya, n)
        if o:
            firsts.append(
                send(ya.at[n], r1a.at[n], s1_sem.at[1, n], r1_sem.at[1, n], (d, x * 4 + shift(y, o, 4)))
            )
    for copy in firsts:
        copy.wait()

    def total(own, got, at):
        return own[3, at] + got[0, at] + (got[1, at] + got[2, at])

    seconds = []
    for n, o in enumerate(ORDER):
        yy, xx = shift(y, o, 4), shift(x, o, 4)
        s2g[n] = total(yg, r1g, yy)
        seconds.append(send(s2g.at[n], r2g.at[n], s2_sem.at[0, n], r2_sem.at[0, n], (d, x * 4 + yy)))
        s2a[n] = total(ya, r1a, xx)
        seconds.append(send(s2a.at[n], r2a.at[n], s2_sem.at[1, n], r2_sem.at[1, n], (d, xx * 4 + y)))
    pg = total(yg, r1g, y)
    pa = total(ya, r1a, x)
    for copy in seconds:
        copy.wait()
    pg = pg + r2g[0] + (r2g[1] + r2g[2])
    pa = pa + r2a[0] + (r2a[1] + r2a[2])
    for s in range(4):
        gh, gl = parts(pg[32 * s : 32 * s + 32].T)
        ah, al = parts(pa[32 * s : 32 * s + 32])
        feature = mm(gh, ah, NN) + mm(gh, al, NN) + mm(gl, ah, NN)
        fsend[:, s] = feature.reshape(16, 8, 128)
    for n in range(15):
        to = shift(t, n + 1, 16)
        copies.append(send(fsend.at[to], frecv.at[t], sf_sem.at[n], rf_sem.at[n], (d, to)))
    frecv[t] = fsend[t]
    for copy in copies:
        copy.wait()
    for k in range(8):
        fd[k] = frecv[:, :, k, :].reshape(64, 128)


def project(act, grad, pin, pout, q, damp):
    sem = pltpu.SemaphoreType.DMA
    return pl.pallas_call(
        project_kernel,
        out_shape=(
            jax.ShapeDtypeStruct((8, 64, 128), F32),
            jax.ShapeDtypeStruct((16, 40, 128), F32),
        ),
        in_specs=[hbm(), hbm(), vmem(), vmem(), vmem(), vmem()],
        out_specs=(vmem(), vmem()),
        scratch_shapes=[
            pltpu.VMEM((4, 4, 128, 1024), F32),
            pltpu.VMEM((4, 4, 128, 1024), F32),
            pltpu.VMEM((1024, 256), BF16),
            pltpu.VMEM((1024, 256), BF16),
            pltpu.VMEM((4, 4, 128, 128), F32),
            pltpu.VMEM((4, 4, 128, 128), F32),
            pltpu.VMEM((3, 4, 128, 128), F32),
            pltpu.VMEM((3, 4, 128, 128), F32),
            pltpu.VMEM((3, 128, 128), F32),
            pltpu.VMEM((3, 128, 128), F32),
            pltpu.VMEM((3, 128, 128), F32),
            pltpu.VMEM((3, 128, 128), F32),
            pltpu.VMEM((16, 40, 128), F32),
            pltpu.VMEM((16, 4, 8, 128), F32),
            pltpu.VMEM((16, 4, 8, 128), F32),
            sem((2, 4)),
            sem((2, 3)),
            sem((2, 3)),
            sem((2, 3)),
            sem((2, 3)),
            sem((15,)),
            sem((15,)),
            sem((15,)),
            sem((15,)),
        ],
        compiler_params=params(1, 54),
    )(act, grad, pin, pout, q, damp)


def main_kernel(
    fd, qcols, qr, gram, back,
    rows, cols, slab, ch, cl, rh, rl, qg, pq, got_pq, fq_own, fq_got, fq, fp, got_fp, pt,
    sums, sums_all, damps, mine, bounds, out,
    s1, r1, sc, rc, sx, rx, s3, r3, s_pq, r_pq, s_fq, r_fq, s_fp, r_fp, s_sum, r_sum,
    s_bound, r_bound, s_out, r_out,
):
    d, t, z, c, x, y = place()
    dp_peers = [(shift(d, o, 8), t) for o in range(1, 8)]
    tensor_peers = [(d, shift(t, o, 16)) for o in range(1, 16)]
    xs = [(d, shift(x, o, 4) * 4 + y) for o in ORDER]
    ys = [(d, x * 4 + shift(y, o, 4)) for o in ORDER]
    greet(dp_peers + tensor_peers)
    greeted(22)
    slab_copies = [send(fd.at[peer[0]], slab.at[d], s1.at[n], r1.at[n], peer) for n, peer in enumerate(dp_peers)]
    zs = [send(fd, cols.at[d], sc.at[n], rc.at[n], (shift(z, o, 4) * 2 + c, t)) for n, o in enumerate(ORDER)]
    other = (z * 2 + 1 - c, t)
    cores = [send(fd, cols.at[d], sx.at[3], rx.at[3], other)]
    slab[d] = fd[d]
    cols[d] = fd[...]

    product = jnp.zeros((64, 512), F32)
    for k in range(4):
        value = jnp.concatenate((fd[2 * k], fd[2 * k + 1]), axis=1)
        high, low = parts(qcols[2 * k : 2 * k + 2].reshape(256, 512))
        product = product + few_rows(value, high, low, NN)
    turned = product.T
    for n in range(16):
        pq[n] = jnp.concatenate((turned[32 * n : 32 * n + 16], turned[32 * n + 16 : 32 * n + 32]), axis=1)

    for copy in slab_copies:
        copy.wait()
    for n in range(4):
        piece = slab[2 * n : 2 * n + 2].reshape(128, 128).T
        rows[t, 0, :, 128 * n : 128 * n + 128] = piece[:64]
        rows[t, 1, :, 128 * n : 128 * n + 128] = piece[64:]

    def hop(half, at, first, second, peer):
        return send(
            rows.at[at, half], rows.at[at, half], s3.at[half, first, second], r3.at[half, first, second], peer
        )

    firsts, rest = {}, []
    for n in range(3):
        firsts[0, n] = hop(0, t, n, 3, xs[n])
        firsts[1, n] = hop(1, t, n, 3, ys[n])
    pq_copies = [
        send(pq.at[peer[1]], got_pq.at[n], s_pq.at[n], r_pq.at[n], peer) for n, peer in enumerate(tensor_peers)
    ]
    for n in range(3):
        rest.append(hop(0, t, 3, n, ys[n]))
        rest.append(hop(1, t, 3, n, xs[n]))

    def source(half, p, n):
        back_by = jnp.where(n == 0, 3, jnp.where(n == 1, 1, jnp.where(n == 2, 2, 0)))
        if half == 0:
            return p * 4 + shift(y, back_by, 4)
        return shift(x, back_by, 4) * 4 + p

    sums[...] = jnp.zeros_like(sums)
    damps[...] = jnp.zeros_like(damps)
    for at in range(16):
        for half in range(2):
            lane = 64 * ((at // 4 if half == 0 else at % 4) % 2)
            damps[2 * at + half : 2 * at + half + 1, lane : lane + 64] = qr[at, 32:33, 64 * half : 64 * half + 64]
    for half in range(2):
        for n in range(4):
            qg[half, n] = jnp.concatenate(
                [qr[source(half, p, n), :, 64 * half : 64 * half + 64] for p in range(4)], axis=1
            )

    for n, o in enumerate(ORDER):
        firsts[0, n].wait()
        for m in range(3):
            rest.append(hop(0, shift(x, 4 - o, 4) * 4 + y, n, m, ys[m]))
        firsts[1, n].wait()
        for m in range(3):
            rest.append(hop(1, x * 4 + shift(y, 4 - o, 4), n, m, xs[m]))
    for copy in pq_copies:
        copy.wait()
    part = pq[t]
    for n in range(15):
        part = part + got_pq[n]
    fq_own[...] = part
    fq_copies = [send(fq_own, fq_got.at[d], s_fq.at[n], r_fq.at[n], peer) for n, peer in enumerate(dp_peers)]
    fq_got[d] = part
    for n, o in enumerate(ORDER):
        zs[n].wait()
        from_d = shift(z, 4 - o, 4) * 2 + c
        cores.append(send(cols.at[from_d], cols.at[from_d], sx.at[n], rx.at[n], other))
    for copy in fq_copies:
        copy.wait()
    for n in range(8):
        fq[:16, 64 * n : 64 * n + 64] = fq_got[n, :, :64]
        fq[16:, 64 * n : 64 * n + 64] = fq_got[n, :, 64:]
    fp[...] = jnp.zeros_like(fp)
    for copy in cores:
        copy.wait()

    def fill(n, carry):
        at = pl.ds(pl.multiple_of(n * 64, 64), 64)
        for k in range(8):
            high, low = parts(cols[n, k] * (1.0 / 512))
            ch[at, 128 * k : 128 * k + 128] = high
            cl[at, 128 * k : 128 * k + 128] = low
        return carry

    lax.fori_loop(0, 8, fill, 0)

    def group(half, n):
        sources = [source(half, p, n) for p in range(4)]
        high, low = parts(jnp.concatenate([rows[at, half] for at in sources], axis=0))
        rh[half, n] = high
        rl[half, n] = low
        total = jnp.zeros((256, 128), F32)
        for k in range(4):
            at = pl.ds(256 * k, 256)
            tile = mm(high, ch[:, at], NN) + mm(high, cl[:, at], NN) + mm(low, ch[:, at], NN)
            for p, source_at in enumerate(sources):
                down = pl.ds(pl.multiple_of(source_at * 128 + 64 * half, 64), 64)
                gram[down, 2 * k, :] = tile[64 * p : 64 * p + 64, :128]
                gram[down, 2 * k + 1, :] = tile[64 * p : 64 * p + 64, 128:]
            total = total + jnp.abs(tile[:, :128]) + jnp.abs(tile[:, 128:])
        for p in range(0, 4, 2):
            line = jnp.sum(total[64 * p : 64 * p + 128].T, axis=0, keepdims=True)
            sums[pl.ds(2 * sources[p] + half, 1), :64] = line[:, :64]
            sums[pl.ds(2 * sources[p + 1] + half, 1), 64:] = line[:, 64:]
        product = few_rows(fq[...], high, low, NT) * (1.0 / 512)
        value = product + qg[half, n, 32:33] * qg[half, n, :32]
        pt[half, n] = value
        fp[...] += few_rows(value, high, low, NN)

    group(0, 3)
    group(1, 3)

    def arrive(n, carry):
        for half in range(2):
            for first in range(4):
                at = source(half, 0, n)
                pltpu.make_async_remote_copy(
                    src_ref=rows.at[at, half],
                    dst_ref=rows.at[at, half],
                    send_sem=s3.at[half, first, n],
                    recv_sem=r3.at[half, first, n],
                    device_id=(d, t),
                    device_id_type=MESH,
                ).wait_recv()
            group(half, n)
        return carry

    lax.fori_loop(0, 3, arrive, 0)
    sum_copies = [
        send(sums, sums_all.at[n], s_sum.at[n], r_sum.at[n], peer) for n, peer in enumerate(tensor_peers)
    ]
    fp_copies = [send(fp, got_fp.at[n], s_fp.at[n], r_fp.at[n], peer) for n, peer in enumerate(dp_peers)]
    for copy in rest:
        copy.wait_send()
    for copy in sum_copies:
        copy.wait()
    row_sums = sums[...] + damps[...]
    for n in range(15):
        row_sums = row_sums + sums_all[n]
    high = jnp.max(row_sums, axis=(0, 1), keepdims=True)
    low = jnp.min(qr[:, 32:33].reshape(16, 128), axis=(0, 1), keepdims=True)
    mine[:8] = jnp.broadcast_to(high, (8, 128))
    mine[8:] = jnp.broadcast_to(low, (8, 128))
    bound_copies = [
        send(mine, bounds.at[n], s_bound.at[n], r_bound.at[n], peer) for n, peer in enumerate(dp_peers)
    ]
    for copy in fp_copies:
        copy.wait()
    fp_all = fp[...]
    for n in range(7):
        fp_all = fp_all + got_fp[n]
    for copy in bound_copies:
        copy.wait()
    bound_high, bound_low = mine[:1], mine[8:9]
    for n in range(7):
        bound_high = jnp.maximum(bound_high, bounds[n, :1])
        bound_low = jnp.minimum(bound_low, bounds[n, 8:9])
    bound_high = jnp.concatenate((bound_high, bound_high), axis=1)
    bound_low = jnp.concatenate((bound_low, bound_low), axis=1)
    ratio_low = bound_low / bound_high
    center = (1.0 + ratio_low) / 2.0
    half_width = (1.0 - ratio_low) / 2.0
    spread = center / half_width
    ratio = 1.0 / spread
    ratio_next = 1.0 / (2.0 * spread - ratio)
    keep = ratio_next * ratio
    add = 2.0 * ratio_next / half_width
    fp_all = fp_all / jnp.concatenate((bound_high, bound_high), axis=1)

    def finish(n, carry):
        for half in range(2):
            product = few_rows(fp_all, rh[half, n], rl[half, n], NT) * (1.0 / 512)
            query, damp = qg[half, n, :32], qg[half, n, 32:33]
            scaled = pt[half, n] / bound_high
            used = scaled / center
            first = query / center
            residual = query - used
            answer = first + (keep * first + add * residual)
            applied = (product / center + damp * used) / bound_high
            residual = residual - (keep * used + add * (scaled - applied))
            for p in range(4):
                at = source(half, p, n)
                lanes = slice(64 * half, 64 * half + 64)
                out[at, 0, :, lanes] = answer[:, 64 * p : 64 * p + 64]
                out[at, 1, :, lanes] = residual[:, 64 * p : 64 * p + 64]
        return carry

    lax.fori_loop(0, 4, finish, 0)
    copies = []
    for n in range(15):
        to = shift(t, n + 1, 16)
        copies.append(send(out.at[to], back.at[t], s_out.at[n], r_out.at[n], (d, to)))
    back[t] = out[t]

    for copy in copies:
        copy.wait()


def main(fd, qcols, qr):
    sem = pltpu.SemaphoreType.DMA
    return pl.pallas_call(
        main_kernel,
        out_shape=(
            jax.ShapeDtypeStruct((2048, 8, 128), F32),
            jax.ShapeDtypeStruct((16, 2, 32, 128), F32),
        ),
        in_specs=[vmem()] * 3,
        out_specs=(vmem(), vmem()),
        scratch_shapes=[
            pltpu.VMEM((16, 2, 64, 512), F32),
            pltpu.VMEM((8, 8, 64, 128), F32),
            pltpu.VMEM((8, 64, 128), F32),
            pltpu.VMEM((512, 1024), BF16),
            pltpu.VMEM((512, 1024), BF16),
            pltpu.VMEM((2, 4, 256, 512), BF16),
            pltpu.VMEM((2, 4, 256, 512), BF16),
            pltpu.VMEM((2, 4, 40, 256), F32),
            pltpu.VMEM((16, 16, 128), F32),
            pltpu.VMEM((15, 16, 128), F32),
            pltpu.VMEM((16, 128), F32),
            pltpu.VMEM((8, 16, 128), F32),
            pltpu.VMEM((32, 512), F32),
            pltpu.VMEM((32, 512), F32),
            pltpu.VMEM((7, 32, 512), F32),
            pltpu.VMEM((2, 4, 32, 256), F32),
            pltpu.VMEM((32, 128), F32),
            pltpu.VMEM((15, 32, 128), F32),
            pltpu.VMEM((32, 128), F32),
            pltpu.VMEM((16, 128), F32),
            pltpu.VMEM((7, 16, 128), F32),
            pltpu.VMEM((16, 2, 32, 128), F32),
            sem((7,)),
            sem((7,)),
            sem((3,)),
            sem((3,)),
            sem((4,)),
            sem((4,)),
            sem((2, 4, 4)),
            sem((2, 4, 4)),
            sem((15,)),
            sem((15,)),
            sem((7,)),
            sem((7,)),
            sem((7,)),
            sem((7,)),
            sem((15,)),
            sem((15,)),
            sem((7,)),
            sem((7,)),
            sem((15,)),
            sem((15,)),
        ],
        compiler_params=params(2, 36),
    )(fd, qcols, qr)


def finish_kernel(gram, back, out, sol, res, sem):
    copies = []
    for n in range(8):
        copy = pltpu.make_async_copy(gram.at[pl.ds(256 * n, 256)], out.at[pl.ds(256 * n, 256)], sem.at[n])
        copy.start()
        copies.append(copy)
    for n in range(4):
        sol[:, 128 * n : 128 * n + 128] = back[4 * n : 4 * n + 4, 0].reshape(128, 128).T
        res[:, 128 * n : 128 * n + 128] = back[4 * n : 4 * n + 4, 1].reshape(128, 128).T
    for copy in copies:
        copy.wait()


def finish(gram, back):
    return pl.pallas_call(
        finish_kernel,
        out_shape=(
            jax.ShapeDtypeStruct((2048, 8, 128), F32),
            jax.ShapeDtypeStruct((128, 512), F32),
            jax.ShapeDtypeStruct((128, 512), F32),
        ),
        in_specs=[vmem(), vmem()],
        out_specs=(hbm(), vmem(), vmem()),
        scratch_shapes=[pltpu.SemaphoreType.DMA((8,))],
        compiler_params=pltpu.CompilerParams(vmem_limit_bytes=16 * 2**20),
    )(gram, back)


def shards(activations, gradients, proj_in, proj_out, damping, queries):
    act = activations.reshape(4, 4, 128, 1024)
    grad = gradients.reshape(4, 4, 128, 1024)
    qcols = lax.all_gather(queries, "dp")
    fd, qr = project(act, grad, proj_in, proj_out, queries, damping.reshape(1, 128))
    gram, back = main(fd, qcols, qr)
    gram, answer, residual = finish(gram, back)
    return answer, residual, gram


def solution(mesh):
    return jax.shard_map(
        shards,
        mesh=mesh,
        in_specs=(
            P("dp", None, "tensor"),
            P("dp", None, "tensor"),
            P("tensor", None),
            P("tensor", None),
            P(("dp", "tensor")),
            P(("dp", "tensor"), None),
        ),
        out_specs=(P(("dp", "tensor"), None), P(("dp", "tensor"), None), P("dp", None, "tensor")),
        check_vma=False,
    )
```

```python
import jax
import jax.numpy as jnp
from jax import lax
from jax.experimental import pallas as pl
from jax.experimental.pallas import tpu as pltpu
from jax.sharding import PartitionSpec as P

MESH = pl.DeviceIdType.MESH
F32 = jnp.float32
BF16 = jnp.bfloat16
ORDER = (1, 3, 2)
NT = (((1,), (1,)), ((), ()))
NN = (((1,), (0,)), ((), ()))
TN = (((0,), (0,)), ((), ()))


def vmem():
    return pl.BlockSpec(memory_space=pltpu.VMEM)


def hbm():
    return pl.BlockSpec(memory_space=pl.ANY)


def params(collective_id, mib):
    return pltpu.CompilerParams(
        collective_id=collective_id, has_side_effects=True, vmem_limit_bytes=mib * 2**20
    )


def place():
    d, t = lax.axis_index("dp"), lax.axis_index("tensor")
    return d, t, lax.div(d, 2), lax.rem(d, 2), lax.div(t, 4), lax.rem(t, 4)


def shift(value, by, size):
    return lax.rem(value + by, size)


def greet(peers):
    barrier = pltpu.get_barrier_semaphore()
    for peer in peers:
        pl.semaphore_signal(barrier, inc=1, device_id=peer, device_id_type=MESH)


def greeted(count):
    pl.semaphore_wait(pltpu.get_barrier_semaphore(), count)


def send(src, dst, send_sem, recv_sem, peer):
    copy = pltpu.make_async_remote_copy(
        src_ref=src,
        dst_ref=dst,
        send_sem=send_sem,
        recv_sem=recv_sem,
        device_id=peer,
        device_id_type=MESH,
    )
    copy.start()
    return copy


def parts(value):
    high = value.astype(BF16)
    low = (value - high.astype(F32)).astype(BF16)
    return high, low


def mm(a, b, dims):
    return lax.dot_general(a, b, dims, preferred_element_type=F32)


def few_rows(value, weight_high, weight_low, dims):
    rows = value.shape[0]
    high, low = parts(value)
    both = mm(jnp.concatenate((high, low), axis=0), weight_high, dims)
    return both[:rows] + both[rows:] + mm(high, weight_low, dims)


def main_kernel(
    act, grad, pin_hbm, pout_hbm, q_hbm, damp_hbm, gram, back,
    pin, pout, q, damp, gbuf, abuf, wg, wa, yg, ya, r1g, r1a, s2g, s2a, r2g, r2a, qs, qr, fsend, frecv, fd, qcols,
    rows, cols, slab, ch, cl, rh, rl, qg, pq, got_pq, fq_own, fq_got, fq, fp, got_fp, fp_half, got_half, fp_total,
    sums, sums_all, damps, mine, bounds, out, got_out,
    small_sem, in_sem, s1_sem, r1_sem, s2_sem, r2_sem, sq_sem, rq_sem, sf_sem, rf_sem, sz_sem, rz_sem,
    s1, r1, sc, rc, sx, rx, s3, r3, s_pq, r_pq, s_fq, r_fq, s_fp, r_fp, s_sum, r_sum,
    s_bound, r_bound, s_out, r_out,
):
    d, t, z, c, x, y = place()
    small = []
    for n, (src, dst) in enumerate(((pout_hbm, pout), (pin_hbm, pin), (q_hbm, q), (damp_hbm, damp))):
        copy = pltpu.make_async_copy(src, dst, small_sem.at[n])
        copy.start()
        small.append(copy)
    loads = []
    for n, o in enumerate(ORDER + (0,)):
        g = pltpu.make_async_copy(grad.at[shift(x, o, 4)], gbuf.at[n], in_sem.at[0, n])
        a = pltpu.make_async_copy(act.at[:, shift(y, o, 4)], abuf.at[n], in_sem.at[1, n])
        if n < 2:
            g.start()
            a.start()
        loads.append((g, a))
    dp_peers = [(shift(d, o, 8), t) for o in range(1, 8)]
    tensor_peers = [(d, shift(t, o, 16)) for o in range(1, 16)]
    xs = [(d, shift(x, o, 4) * 4 + y) for o in ORDER]
    ys = [(d, x * 4 + shift(y, o, 4)) for o in ORDER]
    other = (z * 2 + 1 - c, t)
    greet(dp_peers + tensor_peers)
    row = lax.broadcasted_iota(jnp.int32, (128, 128), 0)
    column = lax.broadcasted_iota(jnp.int32, (128, 128), 1)
    order = (row == 16 * lax.rem(column, 8) + lax.div(column, 8)).astype(BF16)
    for copy in small:
        copy.wait()
    high, low = parts(pout[...])
    wg[:, :128] = mm(high, order, NN).astype(BF16)
    wg[:, 128:] = mm(low, order, NN).astype(BF16)
    high, low = parts(pin[...])
    wa[:, :128] = high
    wa[:, 128:] = low
    for n in range(16):
        qs[n, :32] = q[:, pl.ds(128 * (n // 4), 128)].T[32 * (n % 4) : 32 * (n % 4) + 32]
        qs[n, 32:] = jnp.broadcast_to(damp[...], (8, 128))
    qcols[d] = q[...]
    greeted(22)
    copies = []
    q_zs = [send(q, qcols.at[d], sz_sem.at[n], rz_sem.at[n], (shift(z, o, 4) * 2 + c, t)) for n, o in enumerate(ORDER)]
    q_cores = [send(q, qcols.at[d], sz_sem.at[6], rz_sem.at[6], other)]
    for n in range(15):
        to = shift(t, n + 1, 16)
        copies.append(send(qs.at[to], qr.at[t], sq_sem.at[n], rq_sem.at[n], (d, to)))
    qr[t] = qs[t]

    def project(buf, weight, out, n):
        def step(m, carry):
            at = pl.ds(2 * m, 2)
            high, low = parts(buf[n, at].reshape(256, 1024))
            first = mm(high, weight[...], NN)
            second = mm(low, weight[:, :128], NN)
            out[n, at] = (first[:, :128] + first[:, 128:] + second).reshape(2, 128, 128)
            return carry

        lax.fori_loop(0, 2, step, 0)

    firsts = []
    for n, o in enumerate(ORDER + (0,)):
        loads[n][0].wait()
        if n < 2:
            loads[n + 2][0].start()
        project(gbuf, wg, yg, n)
        if o:
            firsts.append(
                send(yg.at[n], r1g.at[n], s1_sem.at[0, n], r1_sem.at[0, n], (d, shift(x, o, 4) * 4 + y))
            )
        loads[n][1].wait()
        if n < 2:
            loads[n + 2][1].start()
        project(abuf, wa, ya, n)
        if o:
            firsts.append(
                send(ya.at[n], r1a.at[n], s1_sem.at[1, n], r1_sem.at[1, n], (d, x * 4 + shift(y, o, 4)))
            )
    for copy in firsts:
        copy.wait()

    def total(own, got, at):
        return own[3, at] + got[0, at] + (got[1, at] + got[2, at])

    seconds = []
    for n, o in enumerate(ORDER):
        yy, xx = shift(y, o, 4), shift(x, o, 4)
        s2g[n] = total(yg, r1g, yy)
        seconds.append(send(s2g.at[n], r2g.at[n], s2_sem.at[0, n], r2_sem.at[0, n], (d, x * 4 + yy)))
        s2a[n] = total(ya, r1a, xx)
        seconds.append(send(s2a.at[n], r2a.at[n], s2_sem.at[1, n], r2_sem.at[1, n], (d, xx * 4 + y)))
    pg = total(yg, r1g, y)
    pa = total(ya, r1a, x)
    for copy in seconds:
        copy.wait()
    pg = pg + r2g[0] + (r2g[1] + r2g[2])
    pa = pa + r2a[0] + (r2a[1] + r2a[2])
    for s in range(4):
        gh, gl = parts(pg[32 * s : 32 * s + 32].T)
        ah, al = parts(pa[32 * s : 32 * s + 32])
        feature = mm(gh, ah, NN) + mm(gh, al, NN) + mm(gl, ah, NN)
        fsend[:, s] = feature.reshape(16, 8, 128)
    for n in range(15):
        to = shift(t, n + 1, 16)
        copies.append(send(fsend.at[to], frecv.at[t], sf_sem.at[n], rf_sem.at[n], (d, to)))
    frecv[t] = fsend[t]
    for n, o in enumerate(ORDER):
        q_zs[n].wait()
        from_d = shift(z, 4 - o, 4) * 2 + c
        q_cores.append(send(qcols.at[from_d], qcols.at[from_d], sz_sem.at[3 + n], rz_sem.at[3 + n], other))
    for copy in copies:
        copy.wait()
    for k in range(8):
        fd[k] = frecv[:, :, k, :].reshape(64, 128)
    slab_copies = [send(fd.at[peer[0]], slab.at[d], s1.at[n], r1.at[n], peer) for n, peer in enumerate(dp_peers)]
    zs = [send(fd, cols.at[d], sc.at[n], rc.at[n], (shift(z, o, 4) * 2 + c, t)) for n, o in enumerate(ORDER)]
    cores = [send(fd, cols.at[d], sx.at[3], rx.at[3], other)]
    slab[d] = fd[d]
    cols[d] = fd[...]

    for copy in q_cores:
        copy.wait()
    product = jnp.zeros((64, 512), F32)
    for k in range(4):
        value = jnp.concatenate((fd[2 * k], fd[2 * k + 1]), axis=1)
        high, low = parts(qcols[2 * k : 2 * k + 2].reshape(256, 512))
        product = product + few_rows(value, high, low, NN)
    turned = product.T
    for n in range(16):
        pq[n] = jnp.concatenate((turned[32 * n : 32 * n + 16], turned[32 * n + 16 : 32 * n + 32]), axis=1)

    for copy in slab_copies:
        copy.wait()
    for n in range(4):
        piece = slab[2 * n : 2 * n + 2].reshape(128, 128).T
        rows[t, 0, :, 128 * n : 128 * n + 128] = piece[:64]
        rows[t, 1, :, 128 * n : 128 * n + 128] = piece[64:]

    def device(half, first, second):
        if half == 0:
            return shift(x, first % 4, 4) * 4 + shift(y, second % 4, 4)
        return shift(x, second % 4, 4) * 4 + shift(y, first % 4, 4)

    def message(half, first, second, part, axis, step):
        at = device(half, first, second)
        to = device(half, step, 0) if axis == 0 else device(half, 0, step)
        seen = ((first - step) % 4, second % 4) if axis == 0 else (first % 4, (second - step) % 4)
        ref = rows.at[at, half] if part is None else rows.at[at, half, pl.ds(32 * part, 32)]
        return pltpu.make_async_remote_copy(
            src_ref=ref,
            dst_ref=ref,
            send_sem=s3.at[half, seen[0], seen[1], part or 0],
            recv_sem=r3.at[half, seen[0], seen[1], part or 0],
            device_id=(d, to),
            device_id_type=MESH,
        )

    rest = []

    def pass_on(half, first, second, part, axis, *steps):
        for step in steps:
            copy = message(half, first, second, part, axis, step)
            copy.start()
            rest.append(copy)

    def arrived(half, first, second, part):
        at = device(half, first, second)
        ref = rows.at[at, half] if part is None else rows.at[at, half, pl.ds(32 * part, 32)]
        pltpu.make_async_remote_copy(
            src_ref=ref,
            dst_ref=ref,
            send_sem=s3.at[half, first % 4, second % 4, part or 0],
            recv_sem=r3.at[half, first % 4, second % 4, part or 0],
            device_id=(d, t),
            device_id_type=MESH,
        ).wait_recv()

    for axis in range(2):
        for half in range(2):
            pass_on(half, 0, 0, None, axis, 1, -1)
    pq_copies = [
        send(pq.at[peer[1]], got_pq.at[n], s_pq.at[n], r_pq.at[n], peer) for n, peer in enumerate(tensor_peers)
    ]
    def source(half, p, n):
        if half == 0:
            return p * 4 + shift(y, n, 4)
        return shift(x, n, 4) * 4 + p

    sums[...] = jnp.zeros_like(sums)
    damps[...] = jnp.zeros_like(damps)
    for at in range(16):
        for half in range(2):
            lane = 64 * ((at // 4 if half == 0 else at % 4) % 2)
            damps[2 * at + half : 2 * at + half + 1, lane : lane + 64] = qr[at, 32:33, 64 * half : 64 * half + 64]
    for half in range(2):
        for n in range(4):
            qg[half, n] = jnp.concatenate(
                [qr[source(half, p, n), :, 64 * half : 64 * half + 64] for p in range(4)], axis=1
            )

    for first in (-1, 1):
        for half in range(2):
            arrived(half, first, 0, None)
            pass_on(half, first, 0, 0 if first < 0 else 1, 0, -first)
            pass_on(half, first, 0, None, 1, 1, -1)
    for second in (-1, 1):
        for half in range(2):
            arrived(half, 0, second, None)
            pass_on(half, 0, second, 0 if second < 0 else 1, 1, -second)
    for part in range(2):
        for half in range(2):
            arrived(half, 2, 0, part)
            pass_on(half, 2, 0, part, 1, 1, -1)
    for copy in pq_copies:
        copy.wait()
    part = pq[t]
    for n in range(15):
        part = part + got_pq[n]
    fq_own[...] = part
    fq_copies = [send(fq_own, fq_got.at[d], s_fq.at[n], r_fq.at[n], peer) for n, peer in enumerate(dp_peers)]
    fq_got[d] = part
    for n, o in enumerate(ORDER):
        zs[n].wait()
        from_d = shift(z, 4 - o, 4) * 2 + c
        cores.append(send(cols.at[from_d], cols.at[from_d], sx.at[n], rx.at[n], other))
    for first in (-1, 1):
        for second in (-1, 1):
            for half in range(2):
                arrived(half, first, second, None)
                pass_on(half, first, second, 0 if second < 0 else 1, 1, -second)
    for copy in fq_copies:
        copy.wait()
    for n in range(8):
        fq[:16, 64 * n : 64 * n + 64] = fq_got[n, :, :64]
        fq[16:, 64 * n : 64 * n + 64] = fq_got[n, :, 64:]
    fp[...] = jnp.zeros_like(fp)
    for copy in cores:
        copy.wait()

    def fill(n, carry):
        at = pl.ds(pl.multiple_of(n * 64, 64), 64)
        for k in range(8):
            high, low = parts(cols[n, k] * (1.0 / 512))
            ch[at, 128 * k : 128 * k + 128] = high
            cl[at, 128 * k : 128 * k + 128] = low
        return carry

    lax.fori_loop(0, 8, fill, 0)

    def group(half, n):
        sources = [source(half, p, n) for p in range(4)]
        high, low = parts(jnp.concatenate([rows[at, half] for at in sources], axis=0))
        rh[half, n] = high
        rl[half, n] = low
        total = jnp.zeros((256, 128), F32)
        for k in range(4):
            at = pl.ds(256 * k, 256)
            tile = mm(high, ch[:, at], NN) + mm(high, cl[:, at], NN) + mm(low, ch[:, at], NN)
            for p, source_at in enumerate(sources):
                down = pl.ds(pl.multiple_of(source_at * 128 + 64 * half, 64), 64)
                gram[down, 2 * k, :] = tile[64 * p : 64 * p + 64, :128]
                gram[down, 2 * k + 1, :] = tile[64 * p : 64 * p + 64, 128:]
            total = total + jnp.abs(tile[:, :128]) + jnp.abs(tile[:, 128:])
        for p in range(0, 4, 2):
            line = jnp.sum(total[64 * p : 64 * p + 128].T, axis=0, keepdims=True)
            sums[pl.ds(2 * sources[p] + half, 1), :64] = line[:, :64]
            sums[pl.ds(2 * sources[p + 1] + half, 1), 64:] = line[:, 64:]
        product = few_rows(fq[...], high, low, NT) * (1.0 / 512)
        value = product + qg[half, n, 32:33] * qg[half, n, :32]
        for p, at in enumerate(sources):
            out[0, at, :, 64 * half : 64 * half + 64] = value[:, 64 * p : 64 * p + 64]
        fp[...] += few_rows(value, high, low, NN)

    def groups(first_step, last_step):
        def step(n, carry):
            group(0, n)
            group(1, n)
            return carry

        lax.fori_loop(first_step, last_step, step, 0)

    for second in (-1, 1):
        for part in range(2):
            for half in range(2):
                arrived(half, 2, second, part)
                if part == (0 if second < 0 else 1):
                    pass_on(half, 2, second, part, 1, -second)
    groups(0, 2)
    groups(3, 4)
    for first in (0, -1, 1, 2):
        for part in range(2):
            for half in range(2):
                arrived(half, first, 2, part)
    groups(2, 3)
    fp_core = send(fp, got_fp, s_fp.at[0], r_fp.at[0], other)
    sum_copies = [
        send(sums, sums_all.at[n], s_sum.at[n], r_sum.at[n], peer) for n, peer in enumerate(tensor_peers)
    ]
    fp_core.wait()
    own_half = pl.ds(pl.multiple_of(16 * c, 16), 16)
    fp_half[...] = fp[own_half] + got_fp[own_half]
    fp_zs = [
        send(fp_half, got_half.at[n], s_fp.at[1 + n], r_fp.at[1 + n], (shift(z, o, 4) * 2 + c, t))
        for n, o in enumerate(ORDER)
    ]
    copies = []
    for n, peer in enumerate(tensor_peers):
        copies.append(send(out.at[0, peer[1]], got_out.at[0, t], s_out.at[0, n], r_out.at[0, n], peer))
    got_out[0, t] = out[0, t]
    for copy in sum_copies:
        copy.wait()
    row_sums = sums[...] + damps[...]
    for n in range(15):
        row_sums = row_sums + sums_all[n]
    high = jnp.max(row_sums, axis=(0, 1), keepdims=True)
    low = jnp.min(qr[:, 32:33].reshape(16, 128), axis=(0, 1), keepdims=True)
    mine[:8] = jnp.broadcast_to(high, (8, 128))
    mine[8:] = jnp.broadcast_to(low, (8, 128))
    bound_copies = [
        send(mine, bounds.at[n], s_bound.at[n], r_bound.at[n], peer) for n, peer in enumerate(dp_peers)
    ]
    for copy in fp_zs:
        copy.wait()
    fp_total[own_half] = fp_half[...] + got_half[0] + (got_half[1] + got_half[2])
    fp_core = send(fp_total.at[own_half], fp_total.at[own_half], s_fp.at[4], r_fp.at[4], other)
    fp_core.wait()
    fp_all = fp_total[...]
    row_bound = mine[:1]
    fp_all = fp_all * (1.0 / 512) / jnp.concatenate([row_bound] * 4, axis=1)

    def finish(n, carry):
        for half in range(2):
            product = few_rows(fp_all, rh[half, n], rl[half, n], NT)
            for p in range(4):
                out[1, source(half, p, n), :, 64 * half : 64 * half + 64] = product[:, 64 * p : 64 * p + 64]
        return carry

    lax.fori_loop(0, 4, finish, 0)
    for n, peer in enumerate(tensor_peers):
        copies.append(send(out.at[1, peer[1]], got_out.at[1, t], s_out.at[1, n], r_out.at[1, n], peer))
    got_out[1, t] = out[1, t]
    for copy in bound_copies:
        copy.wait()
    bound_high, bound_low = row_bound, mine[8:9]
    for n in range(7):
        bound_high = jnp.maximum(bound_high, bounds[n, :1])
        bound_low = jnp.minimum(bound_low, bounds[n, 8:9])
    row_share = row_bound / bound_high
    ratio_low = bound_low / bound_high
    center = (1.0 + ratio_low) / 2.0
    half_width = (1.0 - ratio_low) / 2.0
    spread = center / half_width
    ratio = 1.0 / spread
    ratio_next = 1.0 / (2.0 * spread - ratio)
    keep = ratio_next * ratio
    add = 2.0 * ratio_next / half_width
    for copy in rest:
        copy.wait_send()
    for copy in copies:
        copy.wait()

    def combine(n, carry):
        query, damp_row = qs[n, :32], qs[n, 32:33]
        scaled = got_out[0, n] / bound_high
        used = scaled / center
        first = query / center
        residual = query - used
        back[n, 0] = first + (keep * first + add * residual)
        applied = got_out[1, n] * row_share / center + damp_row * used
        back[n, 1] = residual - (keep * used + add * (scaled - applied / bound_high))
        return carry

    lax.fori_loop(0, 16, combine, 0)


def main(act, grad, pin, pout, q, damp):
    sem = pltpu.SemaphoreType.DMA
    return pl.pallas_call(
        main_kernel,
        out_shape=(
            jax.ShapeDtypeStruct((2048, 8, 128), F32),
            jax.ShapeDtypeStruct((16, 2, 32, 128), F32),
        ),
        in_specs=[hbm()] * 6,
        out_specs=(vmem(), vmem()),
        scratch_shapes=[
            pltpu.VMEM((1024, 128), F32),
            pltpu.VMEM((1024, 128), F32),
            pltpu.VMEM((128, 512), F32),
            pltpu.VMEM((1, 128), F32),
            pltpu.VMEM((4, 4, 128, 1024), F32),
            pltpu.VMEM((4, 4, 128, 1024), F32),
            pltpu.VMEM((1024, 256), BF16),
            pltpu.VMEM((1024, 256), BF16),
            pltpu.VMEM((4, 4, 128, 128), F32),
            pltpu.VMEM((4, 4, 128, 128), F32),
            pltpu.VMEM((3, 4, 128, 128), F32),
            pltpu.VMEM((3, 4, 128, 128), F32),
            pltpu.VMEM((3, 128, 128), F32),
            pltpu.VMEM((3, 128, 128), F32),
            pltpu.VMEM((3, 128, 128), F32),
            pltpu.VMEM((3, 128, 128), F32),
            pltpu.VMEM((16, 40, 128), F32),
            pltpu.VMEM((16, 40, 128), F32),
            pltpu.VMEM((16, 4, 8, 128), F32),
            pltpu.VMEM((16, 4, 8, 128), F32),
            pltpu.VMEM((8, 64, 128), F32),
            pltpu.VMEM((8, 128, 512), F32),
            pltpu.VMEM((16, 2, 64, 512), F32),
            pltpu.VMEM((8, 8, 64, 128), F32),
            pltpu.VMEM((8, 64, 128), F32),
            pltpu.VMEM((512, 1024), BF16),
            pltpu.VMEM((512, 1024), BF16),
            pltpu.VMEM((2, 4, 256, 512), BF16),
            pltpu.VMEM((2, 4, 256, 512), BF16),
            pltpu.VMEM((2, 4, 40, 256), F32),
            pltpu.VMEM((16, 16, 128), F32),
            pltpu.VMEM((15, 16, 128), F32),
            pltpu.VMEM((16, 128), F32),
            pltpu.VMEM((8, 16, 128), F32),
            pltpu.VMEM((32, 512), F32),
            pltpu.VMEM((32, 512), F32),
            pltpu.VMEM((32, 512), F32),
            pltpu.VMEM((16, 512), F32),
            pltpu.VMEM((3, 16, 512), F32),
            pltpu.VMEM((32, 512), F32),
            pltpu.VMEM((32, 128), F32),
            pltpu.VMEM((15, 32, 128), F32),
            pltpu.VMEM((32, 128), F32),
            pltpu.VMEM((16, 128), F32),
            pltpu.VMEM((7, 16, 128), F32),
            pltpu.VMEM((2, 16, 32, 128), F32),
            pltpu.VMEM((2, 16, 32, 128), F32),
            sem((4,)),
            sem((2, 4)),
            sem((2, 3)),
            sem((2, 3)),
            sem((2, 3)),
            sem((2, 3)),
            sem((15,)),
            sem((15,)),
            sem((15,)),
            sem((15,)),
            sem((7,)),
            sem((7,)),
            sem((7,)),
            sem((7,)),
            sem((3,)),
            sem((3,)),
            sem((4,)),
            sem((4,)),
            sem((2, 4, 4, 2)),
            sem((2, 4, 4, 2)),
            sem((15,)),
            sem((15,)),
            sem((7,)),
            sem((7,)),
            sem((7,)),
            sem((7,)),
            sem((15,)),
            sem((15,)),
            sem((7,)),
            sem((7,)),
            sem((2, 15)),
            sem((2, 15)),
        ],
        compiler_params=params(1, 44),
    )(act, grad, pin, pout, q, damp)


def finish_kernel(gram, back, out, sol, res, sem):
    copies = []
    for n in range(8):
        copy = pltpu.make_async_copy(gram.at[pl.ds(256 * n, 256)], out.at[pl.ds(256 * n, 256)], sem.at[n])
        copy.start()
        copies.append(copy)
    for n in range(4):
        sol[:, 128 * n : 128 * n + 128] = back[4 * n : 4 * n + 4, 0].reshape(128, 128).T
        res[:, 128 * n : 128 * n + 128] = back[4 * n : 4 * n + 4, 1].reshape(128, 128).T
    for copy in copies:
        copy.wait()


def finish(gram, back):
    return pl.pallas_call(
        finish_kernel,
        out_shape=(
            jax.ShapeDtypeStruct((2048, 8, 128), F32),
            jax.ShapeDtypeStruct((128, 512), F32),
            jax.ShapeDtypeStruct((128, 512), F32),
        ),
        in_specs=[vmem(), vmem()],
        out_specs=(hbm(), vmem(), vmem()),
        scratch_shapes=[pltpu.SemaphoreType.DMA((8,))],
        compiler_params=pltpu.CompilerParams(vmem_limit_bytes=16 * 2**20),
    )(gram, back)


def shards(activations, gradients, proj_in, proj_out, damping, queries):
    act = activations.reshape(4, 4, 128, 1024)
    grad = gradients.reshape(4, 4, 128, 1024)
    gram, back = main(act, grad, proj_in, proj_out, queries, damping.reshape(1, 128))
    gram, answer, residual = finish(gram, back)
    return answer, residual, gram


def solution(mesh):
    return jax.shard_map(
        shards,
        mesh=mesh,
        in_specs=(
            P("dp", None, "tensor"),
            P("dp", None, "tensor"),
            P("tensor", None),
            P("tensor", None),
            P(("dp", "tensor")),
            P(("dp", "tensor"), None),
        ),
        out_specs=(P(("dp", "tensor"), None), P(("dp", "tensor"), None), P("dp", None, "tensor")),
        check_vma=False,
    )
```

```python
import jax
import jax.numpy as jnp
from jax import lax
from jax.experimental import pallas as pl
from jax.experimental.pallas import tpu as pltpu
from jax.sharding import PartitionSpec as P

MESH = pl.DeviceIdType.MESH
F32 = jnp.float32
BF16 = jnp.bfloat16
ORDER = (1, 3, 2)
NT = (((1,), (1,)), ((), ()))
NN = (((1,), (0,)), ((), ()))
TN = (((0,), (0,)), ((), ()))


def vmem():
    return pl.BlockSpec(memory_space=pltpu.VMEM)


def hbm():
    return pl.BlockSpec(memory_space=pl.ANY)


def params(collective_id, mib):
    return pltpu.CompilerParams(
        collective_id=collective_id, has_side_effects=True, vmem_limit_bytes=mib * 2**20
    )


def place():
    d, t = lax.axis_index("dp"), lax.axis_index("tensor")
    return d, t, lax.div(d, 2), lax.rem(d, 2), lax.div(t, 4), lax.rem(t, 4)


def shift(value, by, size):
    return lax.rem(value + by, size)


def greet(peers):
    barrier = pltpu.get_barrier_semaphore()
    for peer in peers:
        pl.semaphore_signal(barrier, inc=1, device_id=peer, device_id_type=MESH)


def greeted(count):
    pl.semaphore_wait(pltpu.get_barrier_semaphore(), count)


def send(src, dst, send_sem, recv_sem, peer):
    copy = pltpu.make_async_remote_copy(
        src_ref=src,
        dst_ref=dst,
        send_sem=send_sem,
        recv_sem=recv_sem,
        device_id=peer,
        device_id_type=MESH,
    )
    copy.start()
    return copy


def parts(value):
    high = value.astype(BF16)
    low = (value - high.astype(F32)).astype(BF16)
    return high, low


def mm(a, b, dims):
    return lax.dot_general(a, b, dims, preferred_element_type=F32)


def few_rows(value, weight_high, weight_low, dims):
    rows = value.shape[0]
    high, low = parts(value)
    both = mm(jnp.concatenate((high, low), axis=0), weight_high, dims)
    return both[:rows] + both[rows:] + mm(high, weight_low, dims)


def main_kernel(
    act, grad, pin_hbm, pout_hbm, q_hbm, damp_hbm, gram, back,
    pin, pout, q, damp, gbuf, abuf, wg, wa, yg, ya, r1g, r1a, s2g, s2a, r2g, r2a, qs, qr, fsend, frecv, fd, qcols,
    rows, cols, slab, ch, cl, rh, rl, qg, pq, got_pq, fq_own, fq_got, fq, fp, got_fp, fp_half, got_half, fp_total,
    sums, sums_all, damps, mine, bounds, out, got_out,
    small_sem, in_sem, s1_sem, r1_sem, s2_sem, r2_sem, sq_sem, rq_sem, sf_sem, rf_sem, sz_sem, rz_sem,
    s1, r1, sc, rc, sx, rx, s3, r3, s_pq, r_pq, s_fq, r_fq, s_fp, r_fp, s_sum, r_sum,
    s_bound, r_bound, s_out, r_out,
):
    d, t, z, c, x, y = place()
    small = []
    for n, (src, dst) in enumerate(((pout_hbm, pout), (pin_hbm, pin), (q_hbm, q), (damp_hbm, damp))):
        copy = pltpu.make_async_copy(src, dst, small_sem.at[n])
        copy.start()
        small.append(copy)
    loads = []
    for n, o in enumerate(ORDER + (0,)):
        g = pltpu.make_async_copy(grad.at[shift(x, o, 4)], gbuf.at[n], in_sem.at[0, n])
        a = pltpu.make_async_copy(act.at[:, shift(y, o, 4)], abuf.at[n], in_sem.at[1, n])
        if n < 2:
            g.start()
            a.start()
        loads.append((g, a))
    dp_peers = [(shift(d, o, 8), t) for o in range(1, 8)]
    tensor_peers = [(d, shift(t, o, 16)) for o in range(1, 16)]
    xs = [(d, shift(x, o, 4) * 4 + y) for o in ORDER]
    ys = [(d, x * 4 + shift(y, o, 4)) for o in ORDER]
    other = (z * 2 + 1 - c, t)
    greet(dp_peers + tensor_peers)
    row = lax.broadcasted_iota(jnp.int32, (128, 128), 0)
    column = lax.broadcasted_iota(jnp.int32, (128, 128), 1)
    order = (row == 16 * lax.rem(column, 8) + lax.div(column, 8)).astype(BF16)
    for copy in small:
        copy.wait()
    high, low = parts(pout[...])
    wg[:, :128] = mm(high, order, NN).astype(BF16)
    wg[:, 128:] = mm(low, order, NN).astype(BF16)
    high, low = parts(pin[...])
    wa[:, :128] = high
    wa[:, 128:] = low
    for n in range(16):
        qs[n, :32] = q[:, pl.ds(128 * (n // 4), 128)].T[32 * (n % 4) : 32 * (n % 4) + 32]
        qs[n, 32:] = jnp.broadcast_to(damp[...], (8, 128))
    qcols[d] = q[...]
    greeted(22)
    copies = []
    q_zs = [send(q, qcols.at[d], sz_sem.at[n], rz_sem.at[n], (shift(z, o, 4) * 2 + c, t)) for n, o in enumerate(ORDER)]
    q_cores = [send(q, qcols.at[d], sz_sem.at[6], rz_sem.at[6], other)]

    def project(buf, weight, out, n):
        def step(m, carry):
            at = pl.ds(2 * m, 2)
            high, low = parts(buf[n, at].reshape(256, 1024))
            first = mm(high, weight[...], NN)
            second = mm(low, weight[:, :128], NN)
            out[n, at] = (first[:, :128] + first[:, 128:] + second).reshape(2, 128, 128)
            return carry

        lax.fori_loop(0, 2, step, 0)

    firsts = []
    for n, o in enumerate(ORDER + (0,)):
        loads[n][0].wait()
        if n < 2:
            loads[n + 2][0].start()
        project(gbuf, wg, yg, n)
        if o:
            firsts.append(
                send(yg.at[n], r1g.at[n], s1_sem.at[0, n], r1_sem.at[0, n], (d, shift(x, o, 4) * 4 + y))
            )
        loads[n][1].wait()
        if n < 2:
            loads[n + 2][1].start()
        project(abuf, wa, ya, n)
        if o:
            firsts.append(
                send(ya.at[n], r1a.at[n], s1_sem.at[1, n], r1_sem.at[1, n], (d, x * 4 + shift(y, o, 4)))
            )

    def total(own, got, at):
        return own[3, at] + got[0, at] + (got[1, at] + got[2, at])

    seconds = []
    for copy in firsts[::2]:
        copy.wait_recv()
    for n, o in enumerate(ORDER):
        yy = shift(y, o, 4)
        s2g[n] = total(yg, r1g, yy)
        seconds.append(send(s2g.at[n], r2g.at[n], s2_sem.at[0, n], r2_sem.at[0, n], (d, x * 4 + yy)))
    for copy in firsts[1::2]:
        copy.wait_recv()
    for n, o in enumerate(ORDER):
        xx = shift(x, o, 4)
        s2a[n] = total(ya, r1a, xx)
        seconds.append(send(s2a.at[n], r2a.at[n], s2_sem.at[1, n], r2_sem.at[1, n], (d, xx * 4 + y)))
    pg = total(yg, r1g, y)
    pa = total(ya, r1a, x)
    for copy in firsts:
        copy.wait_send()
    for copy in seconds:
        copy.wait()
    pg = pg + r2g[0] + (r2g[1] + r2g[2])
    pa = pa + r2a[0] + (r2a[1] + r2a[2])
    for s in range(4):
        gh, gl = parts(pg[32 * s : 32 * s + 32].T)
        ah, al = parts(pa[32 * s : 32 * s + 32])
        feature = mm(gh, ah, NN) + mm(gh, al, NN) + mm(gl, ah, NN)
        fsend[:, s] = feature.reshape(16, 8, 128)
    for n in range(15):
        to = shift(t, n + 1, 16)
        copies.append(send(fsend.at[to], frecv.at[t], sf_sem.at[n], rf_sem.at[n], (d, to)))
    frecv[t] = fsend[t]
    for n, o in enumerate(ORDER):
        q_zs[n].wait()
        from_d = shift(z, 4 - o, 4) * 2 + c
        q_cores.append(send(qcols.at[from_d], qcols.at[from_d], sz_sem.at[3 + n], rz_sem.at[3 + n], other))
    for copy in copies:
        copy.wait()
    for k in range(8):
        fd[k] = frecv[:, :, k, :].reshape(64, 128)
    query_copies = []
    slab_copies = [send(fd.at[peer[0]], slab.at[d], s1.at[n], r1.at[n], peer) for n, peer in enumerate(dp_peers)]
    zs = [send(fd, cols.at[d], sc.at[n], rc.at[n], (shift(z, o, 4) * 2 + c, t)) for n, o in enumerate(ORDER)]
    cores = [send(fd, cols.at[d], sx.at[3], rx.at[3], other)]
    for n in range(15):
        to = shift(t, n + 1, 16)
        query_copies.append(send(qs.at[to], qr.at[t], sq_sem.at[n], rq_sem.at[n], (d, to)))
    qr[t] = qs[t]
    slab[d] = fd[d]
    cols[d] = fd[...]

    for copy in q_cores:
        copy.wait()
    product = jnp.zeros((64, 512), F32)
    for k in range(4):
        value = jnp.concatenate((fd[2 * k], fd[2 * k + 1]), axis=1)
        high, low = parts(qcols[2 * k : 2 * k + 2].reshape(256, 512))
        product = product + few_rows(value, high, low, NN)
    turned = product.T
    for n in range(16):
        pq[n] = jnp.concatenate((turned[32 * n : 32 * n + 16], turned[32 * n + 16 : 32 * n + 32]), axis=1)

    for copy in slab_copies:
        copy.wait()
    for n in range(4):
        piece = slab[2 * n : 2 * n + 2].reshape(128, 128).T
        rows[t, 0, :, 128 * n : 128 * n + 128] = piece[:64]
        rows[t, 1, :, 128 * n : 128 * n + 128] = piece[64:]

    def device(half, first, second):
        if half == 0:
            return shift(x, first % 4, 4) * 4 + shift(y, second % 4, 4)
        return shift(x, second % 4, 4) * 4 + shift(y, first % 4, 4)

    def message(half, first, second, part, axis, step):
        at = device(half, first, second)
        to = device(half, step, 0) if axis == 0 else device(half, 0, step)
        seen = ((first - step) % 4, second % 4) if axis == 0 else (first % 4, (second - step) % 4)
        ref = rows.at[at, half] if part is None else rows.at[at, half, pl.ds(32 * part, 32)]
        return pltpu.make_async_remote_copy(
            src_ref=ref,
            dst_ref=ref,
            send_sem=s3.at[half, seen[0], seen[1], part or 0],
            recv_sem=r3.at[half, seen[0], seen[1], part or 0],
            device_id=(d, to),
            device_id_type=MESH,
        )

    rest = []

    def pass_on(half, first, second, part, axis, *steps):
        for step in steps:
            copy = message(half, first, second, part, axis, step)
            copy.start()
            rest.append(copy)

    def arrived(half, first, second, part):
        at = device(half, first, second)
        ref = rows.at[at, half] if part is None else rows.at[at, half, pl.ds(32 * part, 32)]
        pltpu.make_async_remote_copy(
            src_ref=ref,
            dst_ref=ref,
            send_sem=s3.at[half, first % 4, second % 4, part or 0],
            recv_sem=r3.at[half, first % 4, second % 4, part or 0],
            device_id=(d, t),
            device_id_type=MESH,
        ).wait_recv()

    for axis in range(2):
        for half in range(2):
            pass_on(half, 0, 0, None, axis, 1, -1)
    pq_copies = [
        send(pq.at[peer[1]], got_pq.at[n], s_pq.at[n], r_pq.at[n], peer) for n, peer in enumerate(tensor_peers)
    ]
    def source(half, p, n):
        if half == 0:
            return p * 4 + shift(y, n, 4)
        return shift(x, n, 4) * 4 + p

    for copy in query_copies:
        copy.wait()
    sums[...] = jnp.zeros_like(sums)
    damps[...] = jnp.zeros_like(damps)
    for at in range(16):
        for half in range(2):
            lane = 64 * ((at // 4 if half == 0 else at % 4) % 2)
            damps[2 * at + half : 2 * at + half + 1, lane : lane + 64] = qr[at, 32:33, 64 * half : 64 * half + 64]
    for half in range(2):
        for n in range(4):
            qg[half, n] = jnp.concatenate(
                [qr[source(half, p, n), :, 64 * half : 64 * half + 64] for p in range(4)], axis=1
            )

    for first in (-1, 1):
        for half in range(2):
            arrived(half, first, 0, None)
            pass_on(half, first, 0, 0 if first < 0 else 1, 0, -first)
            pass_on(half, first, 0, None, 1, 1, -1)
    for second in (-1, 1):
        for half in range(2):
            arrived(half, 0, second, None)
            pass_on(half, 0, second, 0 if second < 0 else 1, 1, -second)
    for part in range(2):
        for half in range(2):
            arrived(half, 2, 0, part)
            pass_on(half, 2, 0, part, 1, 1, -1)
    for copy in pq_copies:
        copy.wait()
    part = pq[t]
    for n in range(15):
        part = part + got_pq[n]
    fq_own[...] = part
    fq_copies = [send(fq_own, fq_got.at[d], s_fq.at[n], r_fq.at[n], peer) for n, peer in enumerate(dp_peers)]
    fq_got[d] = part
    for n, o in enumerate(ORDER):
        zs[n].wait()
        from_d = shift(z, 4 - o, 4) * 2 + c
        cores.append(send(cols.at[from_d], cols.at[from_d], sx.at[n], rx.at[n], other))
    for copy in cores:
        copy.wait()

    def fill(n, carry):
        at = pl.ds(pl.multiple_of(n * 64, 64), 64)
        for k in range(8):
            high, low = parts(cols[n, k] * (1.0 / 512))
            ch[at, 128 * k : 128 * k + 128] = high
            cl[at, 128 * k : 128 * k + 128] = low
        return carry

    lax.fori_loop(0, 8, fill, 0)

    def group(half, n):
        sources = [source(half, p, n) for p in range(4)]
        high, low = parts(jnp.concatenate([rows[at, half] for at in sources], axis=0))
        rh[half, n] = high
        rl[half, n] = low
        total = jnp.zeros((256, 128), F32)
        for k in range(4):
            at = pl.ds(256 * k, 256)
            tile = mm(high, ch[:, at], NN) + mm(high, cl[:, at], NN) + mm(low, ch[:, at], NN)
            for p, source_at in enumerate(sources):
                down = pl.ds(pl.multiple_of(source_at * 128 + 64 * half, 64), 64)
                gram[down, 2 * k, :] = tile[64 * p : 64 * p + 64, :128]
                gram[down, 2 * k + 1, :] = tile[64 * p : 64 * p + 64, 128:]
            total = total + jnp.abs(tile[:, :128]) + jnp.abs(tile[:, 128:])
        for p in range(0, 4, 2):
            line = jnp.sum(total[64 * p : 64 * p + 128].T, axis=0, keepdims=True)
            sums[pl.ds(2 * sources[p] + half, 1), :64] = line[:, :64]
            sums[pl.ds(2 * sources[p + 1] + half, 1), 64:] = line[:, 64:]

    def queries_of(half, n):
        sources = [source(half, p, n) for p in range(4)]
        high, low = rh[half, n], rl[half, n]
        product = few_rows(fq[...], high, low, NT) * (1.0 / 512)
        value = product + qg[half, n, 32:33] * qg[half, n, :32]
        for p, at in enumerate(sources):
            out[0, at, :, 64 * half : 64 * half + 64] = value[:, 64 * p : 64 * p + 64]
        fp[...] += few_rows(value, high, low, NN)

    def pass_third(first):
        for second in (-1, 1):
            for half in range(2):
                arrived(half, first, second, None)
                pass_on(half, first, second, 0 if second < 0 else 1, 1, -second)

    def pass_fourth(second):
        for part in range(2):
            for half in range(2):
                arrived(half, 2, second, part)
                if part == (0 if second < 0 else 1):
                    pass_on(half, 2, second, part, 1, -second)

    group(0, 0)
    pass_third(-1)
    group(1, 0)
    pass_third(1)
    for copy in fq_copies:
        copy.wait()
    for n in range(8):
        fq[:16, 64 * n : 64 * n + 64] = fq_got[n, :, :64]
        fq[16:, 64 * n : 64 * n + 64] = fq_got[n, :, 64:]
    fp[...] = jnp.zeros_like(fp)
    pass_fourth(-1)
    group(0, 3)
    pass_fourth(1)
    group(1, 3)
    group(0, 1)
    group(1, 1)

    def query_step(n, carry):
        queries_of(0, n)
        queries_of(1, n)
        return carry

    lax.fori_loop(0, 2, query_step, 0)
    lax.fori_loop(3, 4, query_step, 0)
    for half in range(2):
        for first in (0, -1, 1, 2):
            for part in range(2):
                arrived(half, first, 2, part)
        group(half, 2)
    lax.fori_loop(2, 3, query_step, 0)
    fp_core = send(fp, got_fp, s_fp.at[0], r_fp.at[0], other)
    sum_copies = [
        send(sums, sums_all.at[n], s_sum.at[n], r_sum.at[n], peer) for n, peer in enumerate(tensor_peers)
    ]
    fp_core.wait()
    own_half = pl.ds(pl.multiple_of(16 * c, 16), 16)
    fp_half[...] = fp[own_half] + got_fp[own_half]
    fp_zs = [
        send(fp_half, got_half.at[n], s_fp.at[1 + n], r_fp.at[1 + n], (shift(z, o, 4) * 2 + c, t))
        for n, o in enumerate(ORDER)
    ]
    copies = []
    for n, peer in enumerate(tensor_peers):
        copies.append(send(out.at[0, peer[1]], got_out.at[0, t], s_out.at[0, n], r_out.at[0, n], peer))
    got_out[0, t] = out[0, t]
    for copy in sum_copies:
        copy.wait()
    row_sums = sums[...] + damps[...]
    for n in range(15):
        row_sums = row_sums + sums_all[n]
    high = jnp.max(row_sums, axis=(0, 1), keepdims=True)
    low = jnp.min(qr[:, 32:33].reshape(16, 128), axis=(0, 1), keepdims=True)
    mine[:8] = jnp.broadcast_to(high, (8, 128))
    mine[8:] = jnp.broadcast_to(low, (8, 128))
    bound_copies = [
        send(mine, bounds.at[n], s_bound.at[n], r_bound.at[n], peer) for n, peer in enumerate(dp_peers)
    ]
    for copy in fp_zs:
        copy.wait()
    fp_total[own_half] = fp_half[...] + got_half[0] + (got_half[1] + got_half[2])
    fp_core = send(fp_total.at[own_half], fp_total.at[own_half], s_fp.at[4], r_fp.at[4], other)
    fp_core.wait()
    fp_all = fp_total[...]
    row_bound = mine[:1]
    fp_all = fp_all * (1.0 / 512) / jnp.concatenate([row_bound] * 4, axis=1)

    def finish(n, carry):
        for half in range(2):
            product = few_rows(fp_all, rh[half, n], rl[half, n], NT)
            for p in range(4):
                out[1, source(half, p, n), :, 64 * half : 64 * half + 64] = product[:, 64 * p : 64 * p + 64]
        return carry

    lax.fori_loop(0, 4, finish, 0)
    for n, peer in enumerate(tensor_peers):
        copies.append(send(out.at[1, peer[1]], got_out.at[1, t], s_out.at[1, n], r_out.at[1, n], peer))
    got_out[1, t] = out[1, t]
    for copy in bound_copies:
        copy.wait()
    bound_high, bound_low = row_bound, mine[8:9]
    for n in range(7):
        bound_high = jnp.maximum(bound_high, bounds[n, :1])
        bound_low = jnp.minimum(bound_low, bounds[n, 8:9])
    row_share = row_bound / bound_high
    ratio_low = bound_low / bound_high
    center = (1.0 + ratio_low) / 2.0
    half_width = (1.0 - ratio_low) / 2.0
    spread = center / half_width
    ratio = 1.0 / spread
    ratio_next = 1.0 / (2.0 * spread - ratio)
    keep = ratio_next * ratio
    add = 2.0 * ratio_next / half_width
    for copy in rest:
        copy.wait_send()
    for copy in copies:
        copy.wait()

    def combine(n, carry):
        query, damp_row = qs[n, :32], qs[n, 32:33]
        scaled = got_out[0, n] / bound_high
        used = scaled / center
        first = query / center
        residual = query - used
        back[n, 0] = first + (keep * first + add * residual)
        applied = got_out[1, n] * row_share / center + damp_row * used
        back[n, 1] = residual - (keep * used + add * (scaled - applied / bound_high))
        return carry

    lax.fori_loop(0, 16, combine, 0)


def main(act, grad, pin, pout, q, damp):
    sem = pltpu.SemaphoreType.DMA
    return pl.pallas_call(
        main_kernel,
        out_shape=(
            jax.ShapeDtypeStruct((2048, 8, 128), F32),
            jax.ShapeDtypeStruct((16, 2, 32, 128), F32),
        ),
        in_specs=[hbm()] * 6,
        out_specs=(vmem(), vmem()),
        scratch_shapes=[
            pltpu.VMEM((1024, 128), F32),
            pltpu.VMEM((1024, 128), F32),
            pltpu.VMEM((128, 512), F32),
            pltpu.VMEM((1, 128), F32),
            pltpu.VMEM((4, 4, 128, 1024), F32),
            pltpu.VMEM((4, 4, 128, 1024), F32),
            pltpu.VMEM((1024, 256), BF16),
            pltpu.VMEM((1024, 256), BF16),
            pltpu.VMEM((4, 4, 128, 128), F32),
            pltpu.VMEM((4, 4, 128, 128), F32),
            pltpu.VMEM((3, 4, 128, 128), F32),
            pltpu.VMEM((3, 4, 128, 128), F32),
            pltpu.VMEM((3, 128, 128), F32),
            pltpu.VMEM((3, 128, 128), F32),
            pltpu.VMEM((3, 128, 128), F32),
            pltpu.VMEM((3, 128, 128), F32),
            pltpu.VMEM((16, 40, 128), F32),
            pltpu.VMEM((16, 40, 128), F32),
            pltpu.VMEM((16, 4, 8, 128), F32),
            pltpu.VMEM((16, 4, 8, 128), F32),
            pltpu.VMEM((8, 64, 128), F32),
            pltpu.VMEM((8, 128, 512), F32),
            pltpu.VMEM((16, 2, 64, 512), F32),
            pltpu.VMEM((8, 8, 64, 128), F32),
            pltpu.VMEM((8, 64, 128), F32),
            pltpu.VMEM((512, 1024), BF16),
            pltpu.VMEM((512, 1024), BF16),
            pltpu.VMEM((2, 4, 256, 512), BF16),
            pltpu.VMEM((2, 4, 256, 512), BF16),
            pltpu.VMEM((2, 4, 40, 256), F32),
            pltpu.VMEM((16, 16, 128), F32),
            pltpu.VMEM((15, 16, 128), F32),
            pltpu.VMEM((16, 128), F32),
            pltpu.VMEM((8, 16, 128), F32),
            pltpu.VMEM((32, 512), F32),
            pltpu.VMEM((32, 512), F32),
            pltpu.VMEM((32, 512), F32),
            pltpu.VMEM((16, 512), F32),
            pltpu.VMEM((3, 16, 512), F32),
            pltpu.VMEM((32, 512), F32),
            pltpu.VMEM((32, 128), F32),
            pltpu.VMEM((15, 32, 128), F32),
            pltpu.VMEM((32, 128), F32),
            pltpu.VMEM((16, 128), F32),
            pltpu.VMEM((7, 16, 128), F32),
            pltpu.VMEM((2, 16, 32, 128), F32),
            pltpu.VMEM((2, 16, 32, 128), F32),
            sem((4,)),
            sem((2, 4)),
            sem((2, 3)),
            sem((2, 3)),
            sem((2, 3)),
            sem((2, 3)),
            sem((15,)),
            sem((15,)),
            sem((15,)),
            sem((15,)),
            sem((7,)),
            sem((7,)),
            sem((7,)),
            sem((7,)),
            sem((3,)),
            sem((3,)),
            sem((4,)),
            sem((4,)),
            sem((2, 4, 4, 2)),
            sem((2, 4, 4, 2)),
            sem((15,)),
            sem((15,)),
            sem((7,)),
            sem((7,)),
            sem((7,)),
            sem((7,)),
            sem((15,)),
            sem((15,)),
            sem((7,)),
            sem((7,)),
            sem((2, 15)),
            sem((2, 15)),
        ],
        compiler_params=params(1, 44),
    )(act, grad, pin, pout, q, damp)


def finish_kernel(gram, back, out, sol, res, sem):
    copies = []
    for n in range(8):
        copy = pltpu.make_async_copy(gram.at[pl.ds(256 * n, 256)], out.at[pl.ds(256 * n, 256)], sem.at[n])
        copy.start()
        copies.append(copy)
    for n in range(4):
        sol[:, 128 * n : 128 * n + 128] = back[4 * n : 4 * n + 4, 0].reshape(128, 128).T
        res[:, 128 * n : 128 * n + 128] = back[4 * n : 4 * n + 4, 1].reshape(128, 128).T
    for copy in copies:
        copy.wait()


def finish(gram, back):
    return pl.pallas_call(
        finish_kernel,
        out_shape=(
            jax.ShapeDtypeStruct((2048, 8, 128), F32),
            jax.ShapeDtypeStruct((128, 512), F32),
            jax.ShapeDtypeStruct((128, 512), F32),
        ),
        in_specs=[vmem(), vmem()],
        out_specs=(hbm(), vmem(), vmem()),
        scratch_shapes=[pltpu.SemaphoreType.DMA((8,))],
        compiler_params=pltpu.CompilerParams(vmem_limit_bytes=16 * 2**20),
    )(gram, back)


def shards(activations, gradients, proj_in, proj_out, damping, queries):
    act = activations.reshape(4, 4, 128, 1024)
    grad = gradients.reshape(4, 4, 128, 1024)
    small = (proj_in, proj_out, queries, damping.reshape(1, 128))
    gram, back = main(act, grad, *(pltpu.with_memory_space_constraint(value, pltpu.HBM) for value in small))
    gram, answer, residual = finish(gram, back)
    return answer, residual, gram


def solution(mesh):
    return jax.shard_map(
        shards,
        mesh=mesh,
        in_specs=(
            P("dp", None, "tensor"),
            P("dp", None, "tensor"),
            P("tensor", None),
            P("tensor", None),
            P(("dp", "tensor")),
            P(("dp", "tensor"), None),
        ),
        out_specs=(P(("dp", "tensor"), None), P(("dp", "tensor"), None), P("dp", None, "tensor")),
        check_vma=False,
    )
```

```python
import jax
import jax.numpy as jnp
from jax import lax
from jax.experimental import pallas as pl
from jax.experimental.pallas import tpu as pltpu
from jax.sharding import PartitionSpec as P

MESH = pl.DeviceIdType.MESH
F32 = jnp.float32
BF16 = jnp.bfloat16
ORDER = (1, 3, 2)
NT = (((1,), (1,)), ((), ()))
NN = (((1,), (0,)), ((), ()))
TN = (((0,), (0,)), ((), ()))


def vmem():
    return pl.BlockSpec(memory_space=pltpu.VMEM)


def hbm():
    return pl.BlockSpec(memory_space=pl.ANY)


def params(collective_id, mib):
    return pltpu.CompilerParams(
        collective_id=collective_id, has_side_effects=True, vmem_limit_bytes=mib * 2**20
    )


def place():
    d, t = lax.axis_index("dp"), lax.axis_index("tensor")
    return d, t, lax.div(d, 2), lax.rem(d, 2), lax.div(t, 4), lax.rem(t, 4)


def shift(value, by, size):
    return lax.rem(value + by, size)


def greet(peers):
    barrier = pltpu.get_barrier_semaphore()
    for peer in peers:
        pl.semaphore_signal(barrier, inc=1, device_id=peer, device_id_type=MESH)


def greeted(count):
    pl.semaphore_wait(pltpu.get_barrier_semaphore(), count)


def send(src, dst, send_sem, recv_sem, peer):
    copy = pltpu.make_async_remote_copy(
        src_ref=src,
        dst_ref=dst,
        send_sem=send_sem,
        recv_sem=recv_sem,
        device_id=peer,
        device_id_type=MESH,
    )
    copy.start()
    return copy


def parts(value):
    high = value.astype(BF16)
    low = (value - high.astype(F32)).astype(BF16)
    return high, low


def mm(a, b, dims):
    return lax.dot_general(a, b, dims, preferred_element_type=F32)


def few_rows(value, weight_high, weight_low, dims):
    rows = value.shape[0]
    high, low = parts(value)
    both = mm(jnp.concatenate((high, low), axis=0), weight_high, dims)
    return both[:rows] + both[rows:] + mm(high, weight_low, dims)


def main_kernel(
    act, grad, pin_hbm, pout_hbm, q_hbm, damp_hbm, gram, back,
    pin, pout, q, damp, gbuf, abuf, wg, wa, yg, ya, r1g, r1a, s2g, s2a, r2g, r2a, qs, qr, fsend, frecv, fd, qcols,
    rows, cols, slab, ch, cl, rh, rl, qg, pq, got_pq, fq_own, fq_got, fq, fp, got_fp, fp_half, got_half, fp_total,
    sums, sums_all, damps, mine, bounds, out, got_out,
    small_sem, in_sem, s1_sem, r1_sem, s2_sem, r2_sem, sq_sem, rq_sem, sf_sem, rf_sem, sz_sem, rz_sem,
    s1, r1, sc, rc, sx, rx, s3, r3, s_pq, r_pq, s_fq, r_fq, s_fp, r_fp, s_sum, r_sum,
    s_bound, r_bound, s_out, r_out,
):
    d, t, z, c, x, y = place()
    small = []
    for n, (src, dst) in enumerate(((pout_hbm, pout), (pin_hbm, pin), (q_hbm, q), (damp_hbm, damp))):
        copy = pltpu.make_async_copy(src, dst, small_sem.at[n])
        copy.start()
        small.append(copy)
    loads = []
    for n, o in enumerate(ORDER + (0,)):
        g = pltpu.make_async_copy(grad.at[shift(x, o, 4)], gbuf.at[n], in_sem.at[0, n])
        a = pltpu.make_async_copy(act.at[:, shift(y, o, 4)], abuf.at[n], in_sem.at[1, n])
        if n < 2:
            g.start()
            a.start()
        loads.append((g, a))
    dp_peers = [(shift(d, o, 8), t) for o in range(1, 8)]
    tensor_peers = [(d, shift(t, o, 16)) for o in range(1, 16)]
    xs = [(d, shift(x, o, 4) * 4 + y) for o in ORDER]
    ys = [(d, x * 4 + shift(y, o, 4)) for o in ORDER]
    other = (z * 2 + 1 - c, t)
    greet(dp_peers + tensor_peers)
    row = lax.broadcasted_iota(jnp.int32, (128, 128), 0)
    column = lax.broadcasted_iota(jnp.int32, (128, 128), 1)
    order = (row == 16 * lax.rem(column, 8) + lax.div(column, 8)).astype(BF16)
    for copy in small:
        copy.wait()
    high, low = parts(pout[...])
    wg[:, :128] = mm(high, order, NN).astype(BF16)
    wg[:, 128:] = mm(low, order, NN).astype(BF16)
    high, low = parts(pin[...])
    wa[:, :128] = high
    wa[:, 128:] = low
    for n in range(16):
        qs[n, :32] = q[:, pl.ds(128 * (n // 4), 128)].T[32 * (n % 4) : 32 * (n % 4) + 32]
        qs[n, 32:] = jnp.broadcast_to(damp[...], (8, 128))
    qcols[d] = q[...]
    greeted(22)
    copies = []
    q_zs = [send(q, qcols.at[d], sz_sem.at[n], rz_sem.at[n], (shift(z, o, 4) * 2 + c, t)) for n, o in enumerate(ORDER)]
    q_cores = [send(q, qcols.at[d], sz_sem.at[6], rz_sem.at[6], other)]

    def project(buf, weight, out, n):
        def step(m, carry):
            at = pl.ds(2 * m, 2)
            high, low = parts(buf[n, at].reshape(256, 1024))
            first = mm(high, weight[...], NN)
            second = mm(low, weight[:, :128], NN)
            out[n, at] = (first[:, :128] + first[:, 128:] + second).reshape(2, 128, 128)
            return carry

        lax.fori_loop(0, 2, step, 0)

    firsts = []
    for n, o in enumerate(ORDER + (0,)):
        loads[n][0].wait()
        if n < 2:
            loads[n + 2][0].start()
        project(gbuf, wg, yg, n)
        if o:
            firsts.append(
                send(yg.at[n], r1g.at[n], s1_sem.at[0, n], r1_sem.at[0, n], (d, shift(x, o, 4) * 4 + y))
            )
        loads[n][1].wait()
        if n < 2:
            loads[n + 2][1].start()
        project(abuf, wa, ya, n)
        if o:
            firsts.append(
                send(ya.at[n], r1a.at[n], s1_sem.at[1, n], r1_sem.at[1, n], (d, x * 4 + shift(y, o, 4)))
            )

    def total(own, got, at):
        return own[3, at] + got[0, at] + (got[1, at] + got[2, at])

    seconds = []
    for copy in firsts[::2]:
        copy.wait_recv()
    for n, o in enumerate(ORDER):
        yy = shift(y, o, 4)
        s2g[n] = total(yg, r1g, yy)
        seconds.append(send(s2g.at[n], r2g.at[n], s2_sem.at[0, n], r2_sem.at[0, n], (d, x * 4 + yy)))
    for copy in firsts[1::2]:
        copy.wait_recv()
    for n, o in enumerate(ORDER):
        xx = shift(x, o, 4)
        s2a[n] = total(ya, r1a, xx)
        seconds.append(send(s2a.at[n], r2a.at[n], s2_sem.at[1, n], r2_sem.at[1, n], (d, xx * 4 + y)))
    pg = total(yg, r1g, y)
    pa = total(ya, r1a, x)
    for copy in firsts:
        copy.wait_send()
    for copy in seconds:
        copy.wait()
    pg = pg + r2g[0] + (r2g[1] + r2g[2])
    pa = pa + r2a[0] + (r2a[1] + r2a[2])
    for s in range(4):
        gh, gl = parts(pg[32 * s : 32 * s + 32].T)
        ah, al = parts(pa[32 * s : 32 * s + 32])
        feature = mm(gh, ah, NN) + mm(gh, al, NN) + mm(gl, ah, NN)
        fsend[:, s] = feature.reshape(16, 8, 128)
    for n in range(15):
        to = shift(t, n + 1, 16)
        copies.append(send(fsend.at[to], frecv.at[t], sf_sem.at[n], rf_sem.at[n], (d, to)))
    frecv[t] = fsend[t]
    for n, o in enumerate(ORDER):
        q_zs[n].wait()
        from_d = shift(z, 4 - o, 4) * 2 + c
        q_cores.append(send(qcols.at[from_d], qcols.at[from_d], sz_sem.at[3 + n], rz_sem.at[3 + n], other))
    for copy in copies:
        copy.wait()
    for k in range(8):
        fd[k] = frecv[:, :, k, :].reshape(64, 128)
    query_copies = []
    slab_copies = [send(fd.at[peer[0]], slab.at[d], s1.at[n], r1.at[n], peer) for n, peer in enumerate(dp_peers)]
    zs = [send(fd, cols.at[d], sc.at[n], rc.at[n], (shift(z, o, 4) * 2 + c, t)) for n, o in enumerate(ORDER)]
    cores = [send(fd, cols.at[d], sx.at[3], rx.at[3], other)]
    for n in range(15):
        to = shift(t, n + 1, 16)
        query_copies.append(send(qs.at[to], qr.at[t], sq_sem.at[n], rq_sem.at[n], (d, to)))
    qr[t] = qs[t]
    slab[d] = fd[d]
    cols[d] = fd[...]

    for copy in q_cores:
        copy.wait()
    product = jnp.zeros((64, 512), F32)
    for k in range(4):
        value = jnp.concatenate((fd[2 * k], fd[2 * k + 1]), axis=1)
        high, low = parts(qcols[2 * k : 2 * k + 2].reshape(256, 512))
        product = product + few_rows(value, high, low, NN)
    turned = product.T
    for n in range(16):
        pq[n] = jnp.concatenate((turned[32 * n : 32 * n + 16], turned[32 * n + 16 : 32 * n + 32]), axis=1)

    for copy in slab_copies:
        copy.wait()
    for n in range(4):
        piece = slab[2 * n : 2 * n + 2].reshape(128, 128).T
        rows[t, 0, :, 128 * n : 128 * n + 128] = piece[:64]
        rows[t, 1, :, 128 * n : 128 * n + 128] = piece[64:]

    def device(half, first, second):
        if half == 0:
            return shift(x, first % 4, 4) * 4 + shift(y, second % 4, 4)
        return shift(x, second % 4, 4) * 4 + shift(y, first % 4, 4)

    def message(half, first, second, part, axis, step):
        at = device(half, first, second)
        to = device(half, step, 0) if axis == 0 else device(half, 0, step)
        seen = ((first - step) % 4, second % 4) if axis == 0 else (first % 4, (second - step) % 4)
        ref = rows.at[at, half] if part is None else rows.at[at, half, pl.ds(32 * part, 32)]
        return pltpu.make_async_remote_copy(
            src_ref=ref,
            dst_ref=ref,
            send_sem=s3.at[half, seen[0], seen[1], part or 0],
            recv_sem=r3.at[half, seen[0], seen[1], part or 0],
            device_id=(d, to),
            device_id_type=MESH,
        )

    rest = []

    def pass_on(half, first, second, part, axis, *steps):
        for step in steps:
            copy = message(half, first, second, part, axis, step)
            copy.start()
            rest.append(copy)

    def arrived(half, first, second, part):
        at = device(half, first, second)
        ref = rows.at[at, half] if part is None else rows.at[at, half, pl.ds(32 * part, 32)]
        pltpu.make_async_remote_copy(
            src_ref=ref,
            dst_ref=ref,
            send_sem=s3.at[half, first % 4, second % 4, part or 0],
            recv_sem=r3.at[half, first % 4, second % 4, part or 0],
            device_id=(d, t),
            device_id_type=MESH,
        ).wait_recv()

    for axis in range(2):
        for half in range(2):
            pass_on(half, 0, 0, None, axis, 1, -1)
    pq_copies = [
        send(pq.at[peer[1]], got_pq.at[n], s_pq.at[n], r_pq.at[n], peer) for n, peer in enumerate(tensor_peers)
    ]
    def source(half, p, n):
        if half == 0:
            return p * 4 + shift(y, n, 4)
        return shift(x, n, 4) * 4 + p

    for first in (-1, 1):
        for half in range(2):
            arrived(half, first, 0, None)
            pass_on(half, first, 0, 0 if first < 0 else 1, 0, -first)
            pass_on(half, first, 0, None, 1, 1, -1)
    for second in (-1, 1):
        for half in range(2):
            arrived(half, 0, second, None)
            pass_on(half, 0, second, 0 if second < 0 else 1, 1, -second)
    for part in range(2):
        for half in range(2):
            arrived(half, 2, 0, part)
            pass_on(half, 2, 0, part, 1, 1, -1)
    for copy in pq_copies:
        copy.wait()
    part = pq[t]
    for n in range(15):
        part = part + got_pq[n]
    fq_own[...] = part
    fq_copies = [send(fq_own, fq_got.at[d], s_fq.at[n], r_fq.at[n], peer) for n, peer in enumerate(dp_peers)]
    fq_got[d] = part
    for n, o in enumerate(ORDER):
        zs[n].wait()
        from_d = shift(z, 4 - o, 4) * 2 + c
        cores.append(send(cols.at[from_d], cols.at[from_d], sx.at[n], rx.at[n], other))
    for copy in query_copies:
        copy.wait()
    sums[...] = jnp.zeros_like(sums)
    damps[...] = jnp.zeros_like(damps)
    for at in range(16):
        for half in range(2):
            lane = 64 * ((at // 4 if half == 0 else at % 4) % 2)
            damps[2 * at + half : 2 * at + half + 1, lane : lane + 64] = qr[at, 32:33, 64 * half : 64 * half + 64]
    for half in range(2):
        for n in range(4):
            qg[half, n] = jnp.concatenate(
                [qr[source(half, p, n), :, 64 * half : 64 * half + 64] for p in range(4)], axis=1
            )

    for copy in cores:
        copy.wait()

    def fill(n, carry):
        at = pl.ds(pl.multiple_of(n * 64, 64), 64)
        for k in range(8):
            high, low = parts(cols[n, k] * (1.0 / 512))
            ch[at, 128 * k : 128 * k + 128] = high
            cl[at, 128 * k : 128 * k + 128] = low
        return carry

    lax.fori_loop(0, 8, fill, 0)

    def group(half, n):
        sources = [source(half, p, n) for p in range(4)]
        high, low = parts(jnp.concatenate([rows[at, half] for at in sources], axis=0))
        rh[half, n] = high
        rl[half, n] = low
        total = jnp.zeros((256, 128), F32)
        for k in range(4):
            at = pl.ds(256 * k, 256)
            tile = mm(high, ch[:, at], NN) + mm(high, cl[:, at], NN) + mm(low, ch[:, at], NN)
            for p, source_at in enumerate(sources):
                down = pl.ds(pl.multiple_of(source_at * 128 + 64 * half, 64), 64)
                gram[down, 2 * k, :] = tile[64 * p : 64 * p + 64, :128]
                gram[down, 2 * k + 1, :] = tile[64 * p : 64 * p + 64, 128:]
            total = total + jnp.abs(tile[:, :128]) + jnp.abs(tile[:, 128:])
        for p in range(0, 4, 2):
            line = jnp.sum(total[64 * p : 64 * p + 128].T, axis=0, keepdims=True)
            sums[pl.ds(2 * sources[p] + half, 1), :64] = line[:, :64]
            sums[pl.ds(2 * sources[p + 1] + half, 1), 64:] = line[:, 64:]

    def queries_of(half, n):
        sources = [source(half, p, n) for p in range(4)]
        high, low = rh[half, n], rl[half, n]
        product = few_rows(fq[...], high, low, NT) * (1.0 / 512)
        value = product + qg[half, n, 32:33] * qg[half, n, :32]
        for p, at in enumerate(sources):
            out[0, at, :, 64 * half : 64 * half + 64] = value[:, 64 * p : 64 * p + 64]
        fp[...] += few_rows(value, high, low, NN)

    def pass_third(first):
        for second in (-1, 1):
            for half in range(2):
                arrived(half, first, second, None)
                pass_on(half, first, second, 0 if second < 0 else 1, 1, -second)

    def pass_fourth(second):
        for part in range(2):
            for half in range(2):
                arrived(half, 2, second, part)
                if part == (0 if second < 0 else 1):
                    pass_on(half, 2, second, part, 1, -second)

    group(0, 0)
    pass_third(-1)
    group(1, 0)
    pass_third(1)
    for copy in fq_copies:
        copy.wait()
    for n in range(8):
        fq[:16, 64 * n : 64 * n + 64] = fq_got[n, :, :64]
        fq[16:, 64 * n : 64 * n + 64] = fq_got[n, :, 64:]
    fp[...] = jnp.zeros_like(fp)
    pass_fourth(-1)
    group(0, 3)
    pass_fourth(1)
    group(1, 3)
    group(0, 1)
    group(1, 1)

    def query_step(n, carry):
        queries_of(0, n)
        queries_of(1, n)
        return carry

    lax.fori_loop(0, 2, query_step, 0)
    lax.fori_loop(3, 4, query_step, 0)
    for half in range(2):
        for first in (0, -1, 1, 2):
            for part in range(2):
                arrived(half, first, 2, part)
        group(half, 2)
    lax.fori_loop(2, 3, query_step, 0)
    fp_core = send(fp, got_fp, s_fp.at[0], r_fp.at[0], other)
    sum_copies = [
        send(sums, sums_all.at[n], s_sum.at[n], r_sum.at[n], peer) for n, peer in enumerate(tensor_peers)
    ]
    fp_core.wait()
    own_half = pl.ds(pl.multiple_of(16 * c, 16), 16)
    fp_half[...] = fp[own_half] + got_fp[own_half]
    fp_zs = [
        send(fp_half, got_half.at[n], s_fp.at[1 + n], r_fp.at[1 + n], (shift(z, o, 4) * 2 + c, t))
        for n, o in enumerate(ORDER)
    ]
    copies = []
    for n, peer in enumerate(tensor_peers):
        copies.append(send(out.at[0, peer[1]], got_out.at[0, t], s_out.at[0, n], r_out.at[0, n], peer))
    got_out[0, t] = out[0, t]
    for copy in sum_copies:
        copy.wait()
    row_sums = sums[...] + damps[...]
    for n in range(15):
        row_sums = row_sums + sums_all[n]
    high = jnp.max(row_sums, axis=(0, 1), keepdims=True)
    low = jnp.min(qr[:, 32:33].reshape(16, 128), axis=(0, 1), keepdims=True)
    mine[:8] = jnp.broadcast_to(high, (8, 128))
    mine[8:] = jnp.broadcast_to(low, (8, 128))
    bound_copies = [
        send(mine, bounds.at[n], s_bound.at[n], r_bound.at[n], peer) for n, peer in enumerate(dp_peers)
    ]
    for copy in fp_zs:
        copy.wait()
    fp_total[own_half] = fp_half[...] + got_half[0] + (got_half[1] + got_half[2])
    fp_core = send(fp_total.at[own_half], fp_total.at[own_half], s_fp.at[4], r_fp.at[4], other)
    fp_core.wait()
    fp_all = fp_total[...]
    row_bound = mine[:1]
    fp_all = fp_all * (1.0 / 512) / jnp.concatenate([row_bound] * 4, axis=1)

    def finish(n, carry):
        for half in range(2):
            product = few_rows(fp_all, rh[half, n], rl[half, n], NT)
            for p in range(4):
                out[1, source(half, p, n), :, 64 * half : 64 * half + 64] = product[:, 64 * p : 64 * p + 64]
        return carry

    lax.fori_loop(0, 4, finish, 0)
    for n, peer in enumerate(tensor_peers):
        copies.append(send(out.at[1, peer[1]], got_out.at[1, t], s_out.at[1, n], r_out.at[1, n], peer))
    got_out[1, t] = out[1, t]
    for copy in bound_copies:
        copy.wait()
    bound_high, bound_low = row_bound, mine[8:9]
    for n in range(7):
        bound_high = jnp.maximum(bound_high, bounds[n, :1])
        bound_low = jnp.minimum(bound_low, bounds[n, 8:9])
    row_share = row_bound / bound_high
    ratio_low = bound_low / bound_high
    center = (1.0 + ratio_low) / 2.0
    half_width = (1.0 - ratio_low) / 2.0
    spread = center / half_width
    ratio = 1.0 / spread
    ratio_next = 1.0 / (2.0 * spread - ratio)
    keep = ratio_next * ratio
    add = 2.0 * ratio_next / half_width
    for copy in rest:
        copy.wait_send()
    for copy in copies:
        copy.wait()

    def combine(n, carry):
        query, damp_row = qs[n, :32], qs[n, 32:33]
        scaled = got_out[0, n] / bound_high
        used = scaled / center
        first = query / center
        residual = query - used
        back[n, 0] = first + (keep * first + add * residual)
        applied = got_out[1, n] * row_share / center + damp_row * used
        back[n, 1] = residual - (keep * used + add * (scaled - applied / bound_high))
        return carry

    lax.fori_loop(0, 16, combine, 0)


def main(act, grad, pin, pout, q, damp):
    sem = pltpu.SemaphoreType.DMA
    return pl.pallas_call(
        main_kernel,
        out_shape=(
            jax.ShapeDtypeStruct((2048, 8, 128), F32),
            jax.ShapeDtypeStruct((16, 2, 32, 128), F32),
        ),
        in_specs=[hbm()] * 6,
        out_specs=(vmem(), vmem()),
        scratch_shapes=[
            pltpu.VMEM((1024, 128), F32),
            pltpu.VMEM((1024, 128), F32),
            pltpu.VMEM((128, 512), F32),
            pltpu.VMEM((1, 128), F32),
            pltpu.VMEM((4, 4, 128, 1024), F32),
            pltpu.VMEM((4, 4, 128, 1024), F32),
            pltpu.VMEM((1024, 256), BF16),
            pltpu.VMEM((1024, 256), BF16),
            pltpu.VMEM((4, 4, 128, 128), F32),
            pltpu.VMEM((4, 4, 128, 128), F32),
            pltpu.VMEM((3, 4, 128, 128), F32),
            pltpu.VMEM((3, 4, 128, 128), F32),
            pltpu.VMEM((3, 128, 128), F32),
            pltpu.VMEM((3, 128, 128), F32),
            pltpu.VMEM((3, 128, 128), F32),
            pltpu.VMEM((3, 128, 128), F32),
            pltpu.VMEM((16, 40, 128), F32),
            pltpu.VMEM((16, 40, 128), F32),
            pltpu.VMEM((16, 4, 8, 128), F32),
            pltpu.VMEM((16, 4, 8, 128), F32),
            pltpu.VMEM((8, 64, 128), F32),
            pltpu.VMEM((8, 128, 512), F32),
            pltpu.VMEM((16, 2, 64, 512), F32),
            pltpu.VMEM((8, 8, 64, 128), F32),
            pltpu.VMEM((8, 64, 128), F32),
            pltpu.VMEM((512, 1024), BF16),
            pltpu.VMEM((512, 1024), BF16),
            pltpu.VMEM((2, 4, 256, 512), BF16),
            pltpu.VMEM((2, 4, 256, 512), BF16),
            pltpu.VMEM((2, 4, 40, 256), F32),
            pltpu.VMEM((16, 16, 128), F32),
            pltpu.VMEM((15, 16, 128), F32),
            pltpu.VMEM((16, 128), F32),
            pltpu.VMEM((8, 16, 128), F32),
            pltpu.VMEM((32, 512), F32),
            pltpu.VMEM((32, 512), F32),
            pltpu.VMEM((32, 512), F32),
            pltpu.VMEM((16, 512), F32),
            pltpu.VMEM((3, 16, 512), F32),
            pltpu.VMEM((32, 512), F32),
            pltpu.VMEM((32, 128), F32),
            pltpu.VMEM((15, 32, 128), F32),
            pltpu.VMEM((32, 128), F32),
            pltpu.VMEM((16, 128), F32),
            pltpu.VMEM((7, 16, 128), F32),
            pltpu.VMEM((2, 16, 32, 128), F32),
            pltpu.VMEM((2, 16, 32, 128), F32),
            sem((4,)),
            sem((2, 4)),
            sem((2, 3)),
            sem((2, 3)),
            sem((2, 3)),
            sem((2, 3)),
            sem((15,)),
            sem((15,)),
            sem((15,)),
            sem((15,)),
            sem((7,)),
            sem((7,)),
            sem((7,)),
            sem((7,)),
            sem((3,)),
            sem((3,)),
            sem((4,)),
            sem((4,)),
            sem((2, 4, 4, 2)),
            sem((2, 4, 4, 2)),
            sem((15,)),
            sem((15,)),
            sem((7,)),
            sem((7,)),
            sem((7,)),
            sem((7,)),
            sem((15,)),
            sem((15,)),
            sem((7,)),
            sem((7,)),
            sem((2, 15)),
            sem((2, 15)),
        ],
        compiler_params=params(1, 44),
    )(act, grad, pin, pout, q, damp)


def finish_kernel(gram, back, out, sol, res, sem):
    copies = []
    for n in range(8):
        copy = pltpu.make_async_copy(gram.at[pl.ds(256 * n, 256)], out.at[pl.ds(256 * n, 256)], sem.at[n])
        copy.start()
        copies.append(copy)
    for n in range(4):
        sol[:, 128 * n : 128 * n + 128] = back[4 * n : 4 * n + 4, 0].reshape(128, 128).T
        res[:, 128 * n : 128 * n + 128] = back[4 * n : 4 * n + 4, 1].reshape(128, 128).T
    for copy in copies:
        copy.wait()


def finish(gram, back):
    return pl.pallas_call(
        finish_kernel,
        out_shape=(
            jax.ShapeDtypeStruct((2048, 8, 128), F32),
            jax.ShapeDtypeStruct((128, 512), F32),
            jax.ShapeDtypeStruct((128, 512), F32),
        ),
        in_specs=[vmem(), vmem()],
        out_specs=(hbm(), vmem(), vmem()),
        scratch_shapes=[pltpu.SemaphoreType.DMA((8,))],
        compiler_params=pltpu.CompilerParams(vmem_limit_bytes=16 * 2**20),
    )(gram, back)


def shards(activations, gradients, proj_in, proj_out, damping, queries):
    act = activations.reshape(4, 4, 128, 1024)
    grad = gradients.reshape(4, 4, 128, 1024)
    small = (proj_in, proj_out, queries, damping.reshape(1, 128))
    gram, back = main(act, grad, *(pltpu.with_memory_space_constraint(value, pltpu.HBM) for value in small))
    gram, answer, residual = finish(gram, back)
    return answer, residual, gram


def solution(mesh):
    return jax.shard_map(
        shards,
        mesh=mesh,
        in_specs=(
            P("dp", None, "tensor"),
            P("dp", None, "tensor"),
            P("tensor", None),
            P("tensor", None),
            P(("dp", "tensor")),
            P(("dp", "tensor"), None),
        ),
        out_specs=(P(("dp", "tensor"), None), P(("dp", "tensor"), None), P("dp", None, "tensor")),
        check_vma=False,
    )
```
